512 devices in a mesh: section: 4 (over x), dp: 32 (over z, core), tensor: 4 (over y).
Axes of the slice: x: 4, y: 4, z: 16, core: 2. Of those that a mesh axis runs over, the one named last changes fastest.
Arguments:
- text_embed: bfloat16 [8192, 3584], P('dp', 'tensor'), may hold values from -6 to 6
- vision: bfloat16 [2048, 2048], P('dp'), may hold values from -6 to 6
- proj_weight: bfloat16 [2048, 3584], P('dp', 'tensor'), may hold values from -0.125 to 0.125
- out_weight: bfloat16 [4, 3584, 3584], P('section', 'dp', 'tensor'), may hold values from -0.09375 to 0.09375
- qk_gain: float32 [4, 3584], P('section', 'tensor'), may hold values from 0.1 to 1.9
- image_counts: int32 [256], P('dp'), may hold values from 4 to 8, as said below
- sample_shard: int32 [256], P('dp'), may hold values from 0 to 31, as said below
- sample_offset: int32 [256], P('dp'), may hold values from 0 to 252, as said below
- embed_grad: bfloat16 [8192, 3584], P('dp', 'tensor'), may hold values from -6 to 6
Outputs:
- section_out: bfloat16 [4, 8192, 3584], P('section', 'dp', 'tensor')
- image_grad: bfloat16 [2048, 3584], P('dp', 'tensor')
The draws below stay inside these ranges and needn't reach their ends.
Inputs may be any that keep to these rules, and one draw needn't show every extreme that they name: `image_counts`: every encoder device has a sample with exactly 8 image rows and one with exactly 4. `sample_shard`: each dp index receives exactly 8 samples; a dp index that sends samples to another sends it exactly 1. `sample_offset`: A sample's image rows lie inside one document of its shard, and each document of a shard holds the image rows of exactly one sample.
All inputs are finite; a program needn't handle non-finite values.
Results may differ from the reference program's by a relative error of at most 0.0095.
Values may be sent and summed in bfloat16 or wider, within the bound.
A program may use at most 64 MiB of HBM per device.

```python
import jax
import jax.numpy as jnp
from jax import lax

D = 3584
HEAD = 128
ENC_D = 2048
SAMP = 8
DOC = 32
SLOT = 8
HEADS = 28
SHARD_ROWS = 256
TOTAL_ROWS = 8192
IMG_ROWS = 2048
N_SECTION = 4
N_DP = 32


def routing_tables(key):
    key_dest, key_local, key_count, key_jitter = jax.random.split(key, 4)
    values = jnp.arange(N_DP, dtype=jnp.int32)
    ranks = jax.random.permutation(key_dest, N_DP).astype(jnp.int32)
    scores = jnp.where(values == N_DP // 2, -3, jnp.where(values == 1, -2, jnp.where(values == N_DP - 1, -1, ranks))).astype(jnp.int32)
    region_shift = jnp.argsort(scores, stable=True).astype(jnp.int32)
    regions = jnp.arange(SAMP, dtype=jnp.int32)
    shift_of_region = region_shift[regions % N_DP]
    local_keys = jax.random.split(key_local, N_DP)
    region_of = jax.vmap(lambda single: jax.random.permutation(single, SAMP))(local_keys).astype(jnp.int32)
    source = jnp.arange(N_DP, dtype=jnp.int32)[:, None]
    shard = (source + shift_of_region[region_of]) % N_DP
    raw_count = jax.random.randint(key_count, (N_DP, SAMP), SLOT // 2, SLOT + 1).astype(jnp.int32)
    count = jnp.where(region_of == 0, SLOT, jnp.where(region_of == SAMP - 1, SLOT // 2, raw_count))
    raw_jitter = jax.random.randint(key_jitter, (N_DP, SAMP), 0, DOC + 1).astype(jnp.int32)
    jitter = raw_jitter % (DOC - count + 1)
    jitter = jnp.where(region_of == 0, 0, jnp.where(region_of == SAMP - 1, DOC - count, jitter))
    offset = region_of * DOC + jitter
    return (shard.reshape(-1).astype(jnp.int32), offset.reshape(-1).astype(jnp.int32), count.reshape(-1).astype(jnp.int32))


def draw_image_counts(key, part):
    tables = routing_tables(key)
    return tables[2]


def draw_sample_shard(key, part):
    tables = routing_tables(key)
    return tables[0]


def draw_sample_offset(key, part):
    tables = routing_tables(key)
    return tables[1]


def block_scale(own_key, extent, cuts, low, high):
    gain, own = 1.0, jax.random.fold_in(own_key, 6)
    for position, shards_of in cuts:
        draws = jnp.exp(jax.random.uniform(jax.random.fold_in(own, position), (shards_of,), jnp.float32, low / len(cuts), high / len(cuts)))
        gain = gain * jnp.repeat(draws, extent[position] // shards_of).reshape([-1 if axis == position else 1 for axis in range(len(extent))])
    return gain


def bell_draw(key, shape, width, reach, cuts=(), kind=jnp.bfloat16):
    loudness = block_scale(key, shape, cuts, -0.22, 0.18) if cuts else 1.0
    result = jax.random.normal(key, shape, jnp.float32) * width * loudness
    return jnp.minimum(jnp.maximum(result, -reach), reach).astype(kind)


def setup_inputs(seed: int = 0) -> dict:
    streams_of = jax.random.split(jax.random.key(seed), 10)
    return {
        "text_embed": bell_draw(streams_of[0], (TOTAL_ROWS, D), 1.0, 6.0, ((0, 32), (1, 4))),
        "vision": bell_draw(streams_of[1], (IMG_ROWS, ENC_D), 1.0, 6.0, ((0, 32),)),
        "proj_weight": bell_draw(streams_of[2], (ENC_D, D), ENC_D ** -0.5, 0.125, ((0, 32), (1, 4))),
        "out_weight": bell_draw(streams_of[3], (N_SECTION, D, D), D ** -0.5, 0.09375, ((0, 4), (1, 32), (2, 4))),
        "qk_gain": jnp.clip(1.0 + 0.18 * jax.random.normal(streams_of[4], (N_SECTION, D), jnp.float32), 0.1, 1.9),
        "image_counts": draw_image_counts(jax.random.fold_in(streams_of[9], 71), 0),
        "sample_shard": draw_sample_shard(jax.random.fold_in(streams_of[9], 71), 0),
        "sample_offset": draw_sample_offset(jax.random.fold_in(streams_of[9], 71), 0),
        "embed_grad": bell_draw(streams_of[8], (TOTAL_ROWS, D), 1.0, 6.0, ((0, 32), (1, 4))),
    }


def attend(hidden, gains):
    rows = hidden.shape[0]
    values = hidden.astype(jnp.float32).reshape(rows // DOC, DOC, HEADS, HEAD)
    square_mean = lax.optimization_barrier(jnp.mean(values * values, axis=-1, keepdims=True))
    normed = values * lax.rsqrt(square_mean + 1e-06) * gains.reshape(HEADS, HEAD)
    scores = jnp.einsum('dqhe,dkhe->dhqk', normed, normed, precision=lax.Precision.HIGHEST) * (2.0 / HEAD)
    query_pos = lax.broadcasted_iota(jnp.int32, (DOC, DOC), 0)
    key_pos = lax.broadcasted_iota(jnp.int32, (DOC, DOC), 1)
    weights = jnp.where(key_pos <= query_pos, jnp.exp(scores), 0.0)
    weights = weights / lax.optimization_barrier(jnp.sum(weights, axis=-1, keepdims=True))
    rounded = lax.optimization_barrier(weights.astype(jnp.bfloat16))
    mixed = jnp.einsum('dhqk,dkhe->dqhe', rounded.astype(jnp.float32), values, precision=lax.Precision.HIGHEST)
    return mixed.reshape(rows, HEADS * HEAD).astype(jnp.bfloat16)

def reference(text_embed, vision, proj_weight, out_weight, qk_gain, image_counts, sample_shard, sample_offset, embed_grad):
    image_embed = jnp.dot(vision, proj_weight, preferred_element_type=jnp.float32).astype(jnp.bfloat16)
    within = jnp.arange(SLOT, dtype=jnp.int32)[None, :]
    target = sample_shard[:, None] * SHARD_ROWS + sample_offset[:, None] + within
    live = within < image_counts[:, None]
    target = jnp.where(live, target, TOTAL_ROWS).astype(jnp.int32).reshape(-1)
    embedded = text_embed.at[target].set(image_embed, mode='drop')
    hidden = embedded
    results = []
    for block in range(N_SECTION):
        mixed = attend(hidden, qk_gain[block])
        total = hidden.astype(jnp.float32) + jnp.dot(mixed, out_weight[block], preferred_element_type=jnp.float32)
        hidden = total.astype(jnp.bfloat16)
        results.append(hidden)
    clamped = jnp.minimum(target, TOTAL_ROWS - 1).astype(jnp.int32)
    picked = jnp.where(live.reshape(-1, 1), embed_grad[clamped], jnp.zeros((), jnp.bfloat16)).astype(jnp.bfloat16)
    return (jnp.stack(results), picked)
```

```python
import jax
import jax.numpy as jnp
from jax import lax
from jax.experimental import pallas as pl
from jax.experimental.pallas import tpu as pltpu
from jax.sharding import PartitionSpec as P

HEAD = 128
DOC = 32
SLOT = 8
ROWS = 32
SECTIONS = 4


def attend(x, gains):
    rows = x.shape[0]
    row = lax.broadcasted_iota(jnp.int32, (rows, rows), 0)
    col = lax.broadcasted_iota(jnp.int32, (rows, rows), 1)
    allowed = (col <= row) & (col // DOC == row // DOC)
    heads = []
    for head in range(x.shape[1] // HEAD):
        values = x[:, head * HEAD : (head + 1) * HEAD]
        widened = values.astype(jnp.float32)
        mean = jnp.mean(widened * widened, axis=-1, keepdims=True)
        gain = gains[:, head * HEAD : (head + 1) * HEAD]
        normed = (widened * lax.rsqrt(mean + 1e-06) * gain).astype(jnp.bfloat16)
        scores = lax.dot_general(
            normed, normed, (((1,), (1,)), ((), ())), preferred_element_type=jnp.float32
        )
        weights = jnp.where(allowed, jnp.exp(scores * (2.0 / HEAD)), 0.0)
        weights = weights / jnp.sum(weights, axis=-1, keepdims=True)
        heads.append(
            jnp.dot(
                weights.astype(jnp.bfloat16), values, preferred_element_type=jnp.float32
            ).astype(jnp.bfloat16)
        )
    return jnp.concatenate(heads, axis=1)


def blocks_kernel(
    embedded, weight, gain, out, hidden, mixed, hidden_sem, mixed_sem, out_sent, mixed_sent
):
    section, tensor = lax.axis_index("section"), lax.axis_index("tensor")
    micros = hidden.shape[0] // ROWS
    peers = mixed.shape[0]
    width = hidden.shape[1]
    following = lax.rem(section + 1, SECTIONS)

    def rows(micro):
        return pl.ds(pl.multiple_of(micro * ROWS, ROWS), ROWS)

    def relay(micro):
        return pltpu.make_async_remote_copy(
            src_ref=out.at[rows(micro)],
            dst_ref=hidden.at[rows(micro)],
            send_sem=out_sent.at[micro],
            recv_sem=hidden_sem.at[micro],
            device_id={"section": following},
            device_id_type=pl.DeviceIdType.MESH,
        )

    def share(micro, step):
        return pltpu.make_async_remote_copy(
            src_ref=mixed.at[tensor, rows(micro)],
            dst_ref=mixed.at[tensor, rows(micro)],
            send_sem=mixed_sent.at[micro, step - 1],
            recv_sem=mixed_sem.at[micro, step - 1],
            device_id={"tensor": lax.rem(tensor + step, peers)},
            device_id_type=pl.DeviceIdType.MESH,
        )

    barrier = pltpu.get_barrier_semaphore()
    for step in range(1, peers):
        pl.semaphore_signal(
            barrier,
            inc=1,
            device_id={"tensor": lax.rem(tensor + step, peers)},
            device_id_type=pl.DeviceIdType.MESH,
        )
    pl.semaphore_signal(
        barrier,
        inc=1,
        device_id={"section": lax.rem(section + SECTIONS - 1, SECTIONS)},
        device_id_type=pl.DeviceIdType.MESH,
    )
    pl.semaphore_wait(barrier, peers)

    @pl.when(section == 0)
    def _():
        hidden[...] = embedded[...]

    def mix(micro):
        @pl.when(section > 0)
        def _():
            relay(micro).wait_recv()

        mixed[tensor, rows(micro)] = attend(hidden[rows(micro)], gain[...])
        for step in range(1, peers):
            share(micro, step).start()

    def project(micro):
        for step in range(1, peers):
            share(micro, step).wait_recv()
        total = hidden[rows(micro)].astype(jnp.float32)
        for peer in range(peers):
            total += jnp.dot(
                mixed[peer, rows(micro)],
                weight[peer * width : (peer + 1) * width],
                preferred_element_type=jnp.float32,
            )
        out[rows(micro)] = total.astype(jnp.bfloat16)

        @pl.when(section < SECTIONS - 1)
        def _():
            relay(micro).start()

    mix(0)

    def step(micro, carry):
        mix(micro)
        project(micro - 1)
        return carry

    lax.fori_loop(1, micros, step, 0)
    project(micros - 1)

    def drain(micro, carry):
        for step in range(1, peers):
            share(micro, step).wait_send()

        @pl.when(section < SECTIONS - 1)
        def _():
            relay(micro).wait_send()

        return carry

    lax.fori_loop(0, micros, drain, 0)


def run_blocks(embedded, weight, gain, peers):
    rows, width = embedded.shape
    micros = rows // ROWS
    vmem = pl.BlockSpec(memory_space=pltpu.VMEM)
    return pl.pallas_call(
        blocks_kernel,
        out_shape=jax.ShapeDtypeStruct((rows, width), jnp.bfloat16),
        in_specs=[vmem] * 3,
        out_specs=vmem,
        scratch_shapes=[
            pltpu.VMEM((rows, width), jnp.bfloat16),
            pltpu.VMEM((peers, rows, width), jnp.bfloat16),
            pltpu.SemaphoreType.DMA((micros,)),
            pltpu.SemaphoreType.DMA((micros, peers - 1)),
            pltpu.SemaphoreType.DMA((micros,)),
            pltpu.SemaphoreType.DMA((micros, peers - 1)),
        ],
        compiler_params=pltpu.CompilerParams(
            collective_id=0, has_side_effects=True, vmem_limit_bytes=40 * 1024 * 1024
        ),
    )(embedded, weight, gain)


def on_device(
    text_embed,
    vision,
    proj_weight,
    out_weight,
    qk_gain,
    image_counts,
    sample_shard,
    sample_offset,
    embed_grad,
):
    out_full, proj_full = (
        lax.all_gather(out_weight[0], "dp", axis=0, tiled=True),
        lax.all_gather(proj_weight, "dp", axis=0, tiled=True),
    )
    gains = qk_gain[0]
    dp_devices = lax.axis_size("dp")
    samples = sample_shard.shape[0]
    pairs = max(1, samples // dp_devices)
    slots = dp_devices * pairs
    width = text_embed.shape[1]
    feature_count = vision.shape[1]
    later = lax.broadcasted_iota(jnp.int32, (samples, samples), 0)
    former = lax.broadcasted_iota(jnp.int32, (samples, samples), 1)
    same_dest = (sample_shard[:, None] == sample_shard[None, :]) & (former < later)
    rank_within = jnp.sum(same_dest.astype(jnp.int32), axis=1)
    slot_index = sample_shard * pairs + rank_within
    select = slot_index[None, :] == lax.broadcasted_iota(jnp.int32, (slots, samples), 0)
    select_mat = select.astype(jnp.bfloat16)
    details = jnp.stack([sample_offset, image_counts], axis=1)
    slot_details = jnp.sum(jnp.where(select[:, :, None], details[None, :, :], 0), axis=1)
    slot_details = slot_details.reshape(dp_devices, pairs, 2)
    raw_rows = vision.reshape(samples, SLOT * feature_count)
    outgoing = jnp.dot(select_mat, raw_rows, preferred_element_type=jnp.float32).astype(
        jnp.bfloat16
    )
    outgoing = outgoing.reshape(dp_devices, pairs * SLOT, feature_count)
    arrived, arrived_details = (
        lax.all_to_all(outgoing, "dp", split_axis=0, concat_axis=0, tiled=True),
        lax.all_to_all(slot_details, "dp", split_axis=0, concat_axis=0, tiled=True),
    )
    flat_rows = arrived.reshape(slots * SLOT, feature_count)
    image_slots = jnp.dot(flat_rows, proj_full, preferred_element_type=jnp.float32).astype(
        jnp.bfloat16
    )
    arrived_details = arrived_details.reshape(slots, 2)
    within = lax.broadcasted_iota(jnp.int32, (slots, SLOT), 1)
    target = jnp.where(
        within < arrived_details[:, 1:2], arrived_details[:, 0:1] + within, -1
    ).reshape(slots * SLOT)
    shard_rows = text_embed.shape[0]
    placing = target[None, :] == lax.broadcasted_iota(jnp.int32, (shard_rows, slots * SLOT), 0)
    placing_mat = placing.astype(jnp.bfloat16)
    image_rows = jnp.dot(placing_mat, image_slots, preferred_element_type=jnp.float32).astype(
        jnp.bfloat16
    )
    embedded = jnp.where(jnp.any(placing, axis=1)[:, None], image_rows, text_embed)
    returned = jnp.dot(placing_mat.T, embed_grad, preferred_element_type=jnp.float32).astype(
        jnp.bfloat16
    )
    returned = lax.all_to_all(
        returned.reshape(dp_devices, pairs * SLOT, width),
        "dp",
        split_axis=0,
        concat_axis=0,
        tiled=True,
    )
    gathered_back = jnp.dot(
        select_mat.T, returned.reshape(slots, SLOT * width), preferred_element_type=jnp.float32
    )
    image_grad = gathered_back.astype(jnp.bfloat16).reshape(samples * SLOT, width)
    outputs = run_blocks(embedded, out_full, gains[None], lax.axis_size("tensor"))
    return (outputs[None], image_grad)


def solution(mesh):
    placed = (
        P("dp", "tensor"),
        P("dp", None),
        P("dp", "tensor"),
        P("section", "dp", "tensor"),
        P("section", "tensor"),
        P("dp"),
        P("dp"),
        P("dp"),
        P("dp", "tensor"),
    )
    return jax.shard_map(
        on_device,
        mesh=mesh,
        in_specs=placed,
        out_specs=(P("section", "dp", "tensor"), P("dp", "tensor")),
        check_vma=False,
    )
```

```python
import jax
import jax.numpy as jnp
from jax import lax
from jax.experimental import pallas as pl
from jax.experimental.pallas import tpu as pltpu
from jax.sharding import PartitionSpec as P

HEAD = 128
DOC = 32
SLOT = 8
SAMP = 8
ROWS = 32
SECTIONS = 4
PEERS = 4
DP = 32
CHIPS = 16
PART = 256
HALF = 128
WEIGHT_CUTS = ((0, 64), (64, 48))
TILES = ((0, 0), (0, 1), (1, 0), (1, 1), (2, 0), (2, 1), (3, 1))
MESH = pl.DeviceIdType.MESH
BF16 = jnp.bfloat16
F32 = jnp.float32


def attend(x, gains):
    rows = x.shape[0]
    row = lax.broadcasted_iota(jnp.int32, (rows, rows), 0)
    col = lax.broadcasted_iota(jnp.int32, (rows, rows), 1)
    allowed = (col <= row) & (col // DOC == row // DOC)
    heads = []
    for head in range(x.shape[1] // HEAD):
        values = x[:, head * HEAD : (head + 1) * HEAD]
        widened = values.astype(jnp.float32)
        mean = jnp.mean(widened * widened, axis=-1, keepdims=True)
        gain = gains[:, head * HEAD : (head + 1) * HEAD]
        normed = (widened * lax.rsqrt(mean + 1e-06) * gain).astype(jnp.bfloat16)
        scores = lax.dot_general(
            normed, normed, (((1,), (1,)), ((), ())), preferred_element_type=jnp.float32
        )
        weights = jnp.where(allowed, jnp.exp(scores * (2.0 / HEAD)), 0.0)
        weights = weights / jnp.sum(weights, axis=-1, keepdims=True)
        heads.append(
            jnp.dot(
                weights.astype(jnp.bfloat16), values, preferred_element_type=jnp.float32
            ).astype(jnp.bfloat16)
        )
    return jnp.concatenate(heads, axis=1)


def iota(shape, dim):
    return lax.broadcasted_iota(jnp.int32, shape, dim)


def spread(index, scalars):
    total = jnp.zeros(index.shape, jnp.int32)
    for i in range(SAMP):
        total = jnp.where(index == i, scalars[i], total)
    return total


def wait_bytes(ref, sem):
    pltpu.make_async_copy(ref, ref, sem).wait()


def whole_kernel(
    text,
    vision,
    proj,
    shard_weight,
    gain,
    counts,
    dests,
    offsets,
    cotangent,
    out,
    image_grad,
    proj_ring,
    weight,
    outgoing,
    arrived,
    compact,
    returning,
    back,
    grads,
    hidden,
    mixed,
    proj_sem,
    proj_near,
    proj_sent,
    weight_sem,
    weight_near,
    weight_sent,
    route_sem,
    route_sent,
    back_sem,
    back_sent,
    compact_sem,
    compact_sent,
    grads_sem,
    grads_sent,
    hidden_sem,
    mixed_sem,
    out_sent,
    mixed_sent,
):
    section, tensor = lax.axis_index("section"), lax.axis_index("tensor")
    me = lax.axis_index("dp")
    chip, core = lax.div(me, 2), lax.rem(me, 2)
    width = hidden.shape[1]
    micros = hidden.shape[0] // ROWS
    following = lax.rem(section + 1, SECTIONS)
    right = lax.rem(chip + 1, CHIPS) * 2 + core
    left = lax.rem(chip + CHIPS - 1, CHIPS) * 2 + core
    near = chip * 2 + 1 - core
    first_column = pl.multiple_of(section * PART - lax.div(section, 3) * HALF, HALF)

    barrier = pltpu.get_barrier_semaphore()
    for device in (right, left, near):
        pl.semaphore_signal(barrier, inc=1, device_id={"dp": device}, device_id_type=MESH)
    for step in range(1, 4):
        pl.semaphore_signal(
            barrier, inc=1, device_id={"tensor": lax.rem(tensor + step, PEERS)}, device_id_type=MESH
        )
        pl.semaphore_signal(
            barrier,
            inc=1,
            device_id={"section": lax.rem(section + step, SECTIONS)},
            device_id_type=MESH,
        )

    dest = [dests[i] for i in range(SAMP)]
    offset = [offsets[i] for i in range(SAMP)]
    count = [counts[i] for i in range(SAMP)]
    table_row, table_lane = iota((2 * SAMP, PART), 0), iota((2 * SAMP, PART), 1)
    table = jnp.where(
        table_row < SAMP,
        spread(table_row, dest),
        jnp.where(
            table_lane < HALF, spread(table_row - SAMP, offset), spread(table_row - SAMP, count)
        ),
    )
    depth = proj.shape[0]
    proj_ring[me, pl.ds(0, depth)] = proj[:, pl.ds(first_column, PART)]
    proj_ring[me, pl.ds(depth, 2 * SAMP)] = table.astype(F32).astype(BF16)
    own = pl.multiple_of(me * shard_weight.shape[0], 16)
    weight[pl.ds(own, shard_weight.shape[0])] = shard_weight[...]
    pl.semaphore_wait(barrier, 9)

    def send(ref, sent, arrival, device):
        pltpu.make_async_remote_copy(
            src_ref=ref,
            dst_ref=ref,
            send_sem=sent,
            recv_sem=arrival,
            device_id={"dp": device},
            device_id_type=MESH,
        ).start()

    def landed(ref, sent, arrival):
        pltpu.make_async_remote_copy(
            src_ref=ref,
            dst_ref=ref,
            send_sem=sent,
            recv_sem=arrival,
            device_id={"dp": near},
            device_id_type=MESH,
        ).wait_recv()

    def proj_block(slot):
        return proj_ring.at[slot]

    def weight_block(slot, cut):
        start = pl.multiple_of(slot * shard_weight.shape[0] + cut[0], 16)
        return weight.at[pl.ds(start, cut[1])]

    def ring_start(block, arrival, sent, near_sem):
        for device in (right, left):
            send(block(me), sent, arrival(me), device)
        send(block(me), sent, near_sem, near)

    def ring_step(hop, block, arrival, sent, near_sem):
        from_left = lax.rem(chip + CHIPS - hop, CHIPS) * 2 + core
        from_right = lax.rem(chip + hop, CHIPS) * 2 + core
        if hop < CHIPS // 2:
            landed(block(from_left), sent, arrival(from_left))
            if hop < CHIPS // 2 - 1:
                send(block(from_left), sent, arrival(from_left), right)
            else:

                @pl.when(core == 0)
                def _():
                    send(block(from_left), sent, arrival(from_left), right)

            landed(block(from_right), sent, arrival(from_right))
            if hop < CHIPS // 2 - 1:
                send(block(from_right), sent, arrival(from_right), left)
            else:

                @pl.when(core == 1)
                def _():
                    send(block(from_right), sent, arrival(from_right), left)

            send(block(from_left), sent, near_sem, near)
            send(block(from_right), sent, near_sem, near)
        else:
            landed(block(from_left), sent, arrival(from_left))
            send(block(from_left), sent, near_sem, near)

    def weight_args(index):
        cut = WEIGHT_CUTS[index]
        return (
            lambda slot: weight_block(slot, cut),
            lambda slot: weight_sem.at[index, slot],
            weight_sent,
            weight_near,
        )

    def weight_step(hop):
        for index in range(len(WEIGHT_CUTS)):
            ring_step(hop, *weight_args(index))

    def proj_step(hop):
        ring_step(hop, *proj_args)

    proj_args = (proj_block, lambda slot: proj_sem.at[slot], proj_sent, proj_near)

    ring_start(*proj_args)
    for index in range(len(WEIGHT_CUTS)):
        ring_start(*weight_args(index))
    proj_step(1)
    proj_step(2)
    weight_step(1)
    proj_step(3)
    proj_step(4)
    proj_step(5)
    weight_step(2)
    proj_step(6)
    proj_step(7)
    proj_step(8)
    wait_bytes(proj_ring.at[pl.ds(0, CHIPS)], proj_near)

    full = proj_ring[:, 0:depth, :].reshape(DP * depth, PART)
    image = jnp.dot(vision[...], full, preferred_element_type=F32).astype(BF16)
    folded = jnp.concatenate([image[:, :HALF], image[:, HALF:]], axis=0)
    place, lane = iota((DP * 16, HALF), 0), iota((DP * 16, HALF), 1)
    lane_sample = lax.shift_right_logical(lane & 63, 3)
    picks = (lax.shift_right_logical(place, 4) == spread(lane_sample, dest)) & (
        (place & 15) == lax.shift_right_logical(lane, 6) * SLOT + (lane & 7)
    )
    slots = jnp.dot(picks.astype(F32).astype(BF16), folded, preferred_element_type=F32)
    outgoing[...] = slots.astype(BF16).reshape(DP, 16, HALF)
    arrived[me] = outgoing[me]

    def scatter(source, target, sent, arrival):
        def one(step, carry):
            device = lax.rem(me + step, DP)
            pltpu.make_async_remote_copy(
                src_ref=source.at[device],
                dst_ref=target.at[me],
                send_sem=sent,
                recv_sem=arrival,
                device_id={"dp": device},
                device_id_type=MESH,
            ).start()
            return carry

        lax.fori_loop(1, DP, one, 0)

    scatter(outgoing, arrived, route_sent, route_sem)
    weight_step(3)

    tables = proj_ring[:, depth : depth + 2 * SAMP, :].astype(F32)
    chosen = jnp.sum(
        jnp.where(tables[:, :SAMP] == me.astype(F32), tables[:, SAMP:], 0.0), axis=1, keepdims=True
    ).astype(jnp.int32)
    start_row, row_count = chosen[:, :, :HALF], chosen[:, :, HALF:]
    shape = (DP, 16, HALF)
    inner, column = iota(shape, 1), iota(shape, 2)
    within = column & 7
    gathers = (
        (lax.shift_right_logical(start_row, 5) == lax.shift_right_logical(column & 63, 3))
        & (inner == lax.shift_right_logical(column, 6) * SLOT + within)
        & (within < row_count)
    )
    gathers = gathers.astype(F32).astype(BF16).reshape(DP * 16, HALF)
    wait_bytes(arrived.at[pl.ds(0, DP - 1)], route_sem)
    packed = lax.dot_general(
        gathers,
        arrived[...].reshape(DP * 16, HALF),
        (((0,), (0,)), ((), ())),
        preferred_element_type=F32,
    )
    compact[section] = packed.astype(BF16)

    def hand_in(source):
        return pltpu.make_async_remote_copy(
            src_ref=compact.at[source],
            dst_ref=compact.at[source],
            send_sem=compact_sent,
            recv_sem=compact_sem.at[source],
            device_id={"section": 0},
            device_id_type=MESH,
        )

    @pl.when(section > 0)
    def _():
        hand_in(section).start()

    weight_step(4)

    @pl.when(section == 0)
    def _():
        for source in range(1, SECTIONS):
            hand_in(source).wait_recv()
        mark = iota((DP, HALF), 1)
        of_doc = lax.shift_right_logical(start_row[:, 0], 5) == lax.shift_right_logical(mark, 3)
        doc_row = jnp.sum(jnp.where(of_doc, start_row[:, 0], 0), axis=0, keepdims=True)
        doc_count = jnp.sum(jnp.where(of_doc, row_count[:, 0], 0), axis=0, keepdims=True)
        rows, mark = iota((text.shape[0], HALF), 0), iota((text.shape[0], HALF), 1)
        puts = (rows == doc_row + (mark & 7)) & ((mark & 7) < doc_count) & (mark < SAMP * SLOT)
        puts = puts.astype(F32)
        taken = jnp.sum(puts, axis=1, keepdims=True) > 0.0
        puts = puts[:, : SAMP * SLOT].astype(BF16)
        for tile, (source, half) in enumerate(TILES):
            columns = slice(tile * HALF, (tile + 1) * HALF)
            rows_here = compact[source, half * SAMP * SLOT : (half + 1) * SAMP * SLOT]
            placed = jnp.dot(puts, rows_here, preferred_element_type=F32)
            hidden[:, columns] = jnp.where(
                taken, placed, text[:, columns].astype(F32)
            ).astype(BF16)

    weight_step(5)

    def send_back():
        shape = (DP, 16, text.shape[0])
        inner, row = iota(shape, 1), iota(shape, 2)
        start = jnp.concatenate([start_row] * (text.shape[0] // HALF), axis=2)
        length = jnp.concatenate([row_count] * (text.shape[0] // HALF), axis=2)
        low = (start + inner == row) & (inner < length)
        high = (start + inner - SLOT == row) & (inner >= SLOT) & (inner - SLOT < length)
        low = low.astype(F32).astype(BF16).reshape(DP * 16, text.shape[0])
        high = high.astype(F32).astype(BF16).reshape(DP * 16, text.shape[0])
        part = cotangent[:, pl.ds(first_column, PART)]
        rows = jnp.dot(low, part[:, :HALF], preferred_element_type=F32)
        rows += jnp.dot(high, part[:, HALF:], preferred_element_type=F32)
        returning[...] = rows.astype(BF16).reshape(DP, 16, HALF)
        back[me] = returning[me]
        scatter(returning, back, back_sent, back_sem)

    def exchange(step):
        return pltpu.make_async_remote_copy(
            src_ref=grads.at[section],
            dst_ref=grads.at[section],
            send_sem=grads_sent.at[step - 1],
            recv_sem=grads_sem.at[step - 1],
            device_id={"section": lax.rem(section + step, SECTIONS)},
            device_id_type=MESH,
        )

    def collect():
        wait_bytes(back.at[pl.ds(0, DP - 1)], back_sem)
        shape = (2 * SAMP * SLOT, DP * 16)
        row, place = iota(shape, 0), iota(shape, 1)
        sample = lax.shift_right_logical(row & 63, 3)
        wants = (lax.shift_right_logical(place, 4) == spread(sample, dest)) & (
            (place & 15) == lax.shift_right_logical(row, 6) * SLOT + (row & 7)
        )
        grads[section] = jnp.dot(
            wants.astype(F32).astype(BF16),
            back[...].reshape(DP * 16, HALF),
            preferred_element_type=F32,
        ).astype(BF16)
        for step in range(1, SECTIONS):
            exchange(step).start()

    def rows_of(micro):
        return pl.ds(pl.multiple_of(micro * ROWS, ROWS), ROWS)

    def relay(micro):
        return pltpu.make_async_remote_copy(
            src_ref=out.at[rows_of(micro)],
            dst_ref=hidden.at[rows_of(micro)],
            send_sem=out_sent.at[micro],
            recv_sem=hidden_sem.at[micro],
            device_id={"section": following},
            device_id_type=MESH,
        )

    def share(micro, step):
        return pltpu.make_async_remote_copy(
            src_ref=mixed.at[tensor, rows_of(micro)],
            dst_ref=mixed.at[tensor, rows_of(micro)],
            send_sem=mixed_sent.at[micro, step - 1],
            recv_sem=mixed_sem.at[micro, step - 1],
            device_id={"tensor": lax.rem(tensor + step, PEERS)},
            device_id_type=MESH,
        )

    def mix(micro):
        mixed[tensor, rows_of(micro)] = attend(hidden[rows_of(micro)], gain[...])
        for step in range(1, PEERS):
            share(micro, step).start()

    def project(micro):
        for step in range(1, PEERS):
            share(micro, step).wait_recv()
        total = hidden[rows_of(micro)].astype(F32)
        for peer in range(PEERS):
            total += jnp.dot(
                mixed[peer, rows_of(micro)],
                weight[peer * width : (peer + 1) * width],
                preferred_element_type=F32,
            )
        out[rows_of(micro)] = total.astype(BF16)

        @pl.when(section < SECTIONS - 1)
        def _():
            relay(micro).start()

    def mix_some(first, last):
        @pl.when(section == 0)
        def _():
            def one(micro, carry):
                mix(micro)
                return carry

            lax.fori_loop(first, last, one, 0)

    mix_some(0, micros // 2)

    @pl.when(section > 0)
    def _():
        send_back()

    weight_step(6)
    mix_some(micros // 2, micros)
    weight_step(7)

    @pl.when(section > 0)
    def _():
        collect()

    weight_step(8)
    wait_bytes(weight.at[pl.ds(0, CHIPS * shard_weight.shape[0])], weight_near)

    def step(turn, carry):
        @pl.when((section > 0) & (turn < micros))
        def _():
            relay(turn).wait_recv()
            mix(turn)

        @pl.when(turn > 0)
        def _():
            project(turn - 1)

        return carry

    lax.fori_loop(0, micros + 1, step, 0)

    @pl.when(section == 0)
    def _():
        send_back()
        collect()

    for step in range(1, SECTIONS):
        exchange(step).wait_recv()
    for tile, (source, half) in enumerate(TILES):
        image_grad[:, tile * HALF : (tile + 1) * HALF] = grads[
            source, half * SAMP * SLOT : (half + 1) * SAMP * SLOT
        ]

    wait_bytes(proj_ring.at[pl.ds(0, DP - 1)], proj_sent)
    wait_bytes(weight.at[pl.ds(0, (DP - 1) * shard_weight.shape[0])], weight_sent)
    wait_bytes(arrived.at[pl.ds(0, DP - 1)], route_sent)
    wait_bytes(arrived.at[pl.ds(0, DP - 1)], back_sent)

    @pl.when(section > 0)
    def _():
        hand_in(section).wait_send()

    for step in range(1, SECTIONS):
        exchange(step).wait_send()

    def drain(micro, carry):
        for step in range(1, PEERS):
            share(micro, step).wait_send()

        @pl.when(section < SECTIONS - 1)
        def _():
            relay(micro).wait_send()

        return carry

    lax.fori_loop(0, micros, drain, 0)


def on_device(
    text_embed,
    vision,
    proj_weight,
    out_weight,
    qk_gain,
    image_counts,
    sample_shard,
    sample_offset,
    embed_grad,
):
    rows, width = text_embed.shape
    micros = rows // ROWS
    depth = proj_weight.shape[0]
    vmem = pl.BlockSpec(memory_space=pltpu.VMEM)
    smem = pl.BlockSpec(memory_space=pltpu.SMEM)
    dma = pltpu.SemaphoreType.DMA
    outputs, image_grad = pl.pallas_call(
        whole_kernel,
        out_shape=(
            jax.ShapeDtypeStruct((rows, width), BF16),
            jax.ShapeDtypeStruct((vision.shape[0], width), BF16),
        ),
        in_specs=[vmem] * 5 + [smem] * 3 + [vmem],
        out_specs=(vmem, vmem),
        scratch_shapes=[
            pltpu.VMEM((DP, depth + 2 * SAMP, PART), BF16),
            pltpu.VMEM((DP * out_weight.shape[1], width), BF16),
            pltpu.VMEM((DP, 16, HALF), BF16),
            pltpu.VMEM((DP, 16, HALF), BF16),
            pltpu.VMEM((SECTIONS, 2 * SAMP * SLOT, HALF), BF16),
            pltpu.VMEM((DP, 16, HALF), BF16),
            pltpu.VMEM((DP, 16, HALF), BF16),
            pltpu.VMEM((SECTIONS, 2 * SAMP * SLOT, HALF), BF16),
            pltpu.VMEM((rows, width), BF16),
            pltpu.VMEM((PEERS, rows, width), BF16),
            dma((DP,)),
            dma,
            dma,
            dma((len(WEIGHT_CUTS), DP)),
            dma,
            dma,
            dma,
            dma,
            dma,
            dma,
            dma((SECTIONS,)),
            dma,
            dma((SECTIONS - 1,)),
            dma((SECTIONS - 1,)),
            dma((micros,)),
            dma((micros, PEERS - 1)),
            dma((micros,)),
            dma((micros, PEERS - 1)),
        ],
        compiler_params=pltpu.CompilerParams(
            collective_id=0, has_side_effects=True, vmem_limit_bytes=40 * 1024 * 1024
        ),
    )(
        text_embed,
        vision,
        proj_weight,
        out_weight[0],
        qk_gain,
        image_counts,
        sample_shard,
        sample_offset,
        embed_grad,
    )
    return (outputs[None], image_grad)


def solution(mesh):
    placed = (
        P("dp", "tensor"),
        P("dp", None),
        P("dp", "tensor"),
        P("section", "dp", "tensor"),
        P("section", "tensor"),
        P("dp"),
        P("dp"),
        P("dp"),
        P("dp", "tensor"),
    )
    return jax.shard_map(
        on_device,
        mesh=mesh,
        in_specs=placed,
        out_specs=(P("section", "dp", "tensor"), P("dp", "tensor")),
        check_vma=False,
    )
```

```python
import jax
import jax.numpy as jnp
from jax import lax
from jax.experimental import pallas as pl
from jax.experimental.pallas import tpu as pltpu
from jax.sharding import PartitionSpec as P

HEAD = 128
DOC = 32
SLOT = 8
SAMP = 8
ROWS = 32
SECTIONS = 4
PEERS = 4
DP = 32
CHIPS = 16
PIECES = 16
HALF = 128
FRONT = 512
FOLDED = 64
PLACERS = 2
WEIGHT_CUTS = ((0, 64), (64, 48))
IMAGE_TILES = ((2, 0), (2, 1), (2, 2), (2, 3), (3, 1), (3, 2), (3, 3))
TILES = ((1, 0), (1, 1), (2, 0), (2, 1), (3, 0), (3, 1), (3, 2))
MESH = pl.DeviceIdType.MESH
BF16 = jnp.bfloat16
F32 = jnp.float32


def attend(x, gains):
    rows = x.shape[0]
    row, col = iota((rows, rows), 0), iota((rows, rows), 1)
    allowed = (col <= row) & (lax.div(col, DOC) == lax.div(row, DOC))
    cuts = [slice(first, first + HEAD) for first in range(0, x.shape[1], HEAD)]
    values = [x[:, cut] for cut in cuts]
    wide = [value.astype(F32) for value in values]
    means = [jnp.mean(value * value, axis=-1, keepdims=True) for value in wide]
    normed = [
        (value * lax.rsqrt(mean + 1e-06) * gains[:, cut]).astype(BF16)
        for value, mean, cut in zip(wide, means, cuts)
    ]
    scores = [
        lax.dot_general(each, each, (((1,), (1,)), ((), ())), preferred_element_type=F32)
        for each in normed
    ]
    weights = [jnp.where(allowed, jnp.exp(score * (2.0 / HEAD)), 0.0) for score in scores]
    weights = [(each / jnp.sum(each, axis=-1, keepdims=True)).astype(BF16) for each in weights]
    mixed = [
        jnp.dot(each, value, preferred_element_type=F32).astype(BF16)
        for each, value in zip(weights, values)
    ]
    return jnp.concatenate(mixed, axis=1)


def iota(shape, dim):
    return lax.broadcasted_iota(jnp.int32, shape, dim)


def spread(index, scalars):
    total = jnp.zeros(index.shape, jnp.int32)
    for i in range(SAMP):
        total = jnp.where(index == i, scalars[i], total)
    return total


def wait_bytes(ref, sem):
    pltpu.make_async_copy(ref, ref, sem).wait()


def whole_kernel(
    text,
    vision,
    proj,
    shard_weight,
    gain_input,
    counts,
    dests,
    offsets,
    cotangent_input,
    out,
    image_grad,
    gain,
    vision_part,
    cotangent,
    proj_ring,
    weight,
    outgoing,
    arrived,
    pieces,
    images,
    returning,
    back,
    hidden,
    mixed,
    load_sem,
    pieces_sem,
    pieces_sent,
    rows_sem,
    rows_sent,
    proj_sem,
    proj_near,
    proj_sent,
    weight_sem,
    weight_near,
    weight_sent,
    route_sem,
    route_sent,
    back_sem,
    back_sent,
    images_sem,
    images_sent,
    grads_sem,
    grads_sent,
    hidden_sem,
    mixed_sem,
    out_sent,
    mixed_sent,
):
    section, tensor = lax.axis_index("section"), lax.axis_index("tensor")
    me = lax.axis_index("dp")
    chip, core = lax.div(me, 2), lax.rem(me, 2)
    width = hidden.shape[1]
    micros = hidden.shape[0] // ROWS
    following = lax.rem(section + 1, SECTIONS)
    right = lax.rem(chip + 1, CHIPS) * 2 + core
    left = lax.rem(chip + CHIPS - 1, CHIPS) * 2 + core
    near = chip * 2 + 1 - core
    image_column = pl.multiple_of(lax.div(section, 3) * 3 * HALF, HALF)
    piece = section * PEERS + tensor
    depth, share_rows = proj.shape[0], shard_weight.shape[0]

    def load(source, target, index):
        return pltpu.make_async_copy(source, target, load_sem.at[index])

    own = pl.multiple_of(me * share_rows, 16)
    load_weight = load(shard_weight, weight.at[pl.ds(own, share_rows)], 0)
    load_vision = load(
        vision.at[:, pl.ds(pl.multiple_of(piece * HALF, HALF), HALF)], vision_part, 1
    )
    load_cotangent = load(cotangent_input, cotangent, 2)
    load_text = load(text, hidden, 3)
    load_proj = load(proj.at[:, pl.ds(image_column, FRONT)], proj_ring.at[me], 4)
    load_gain = load(gain_input, gain, 5)
    load_weight.start()
    load_gain.start()
    load_vision.start()

    @pl.when(section >= PLACERS)
    def _():
        load_proj.start()

    barrier = pltpu.get_barrier_semaphore()

    def greet(step, carry):
        pl.semaphore_signal(
            barrier, inc=1, device_id={"dp": lax.rem(me + step, DP)}, device_id_type=MESH
        )
        return carry

    lax.fori_loop(1, DP, greet, 0)
    for step in range(1, 4):
        pl.semaphore_signal(
            barrier, inc=1, device_id={"tensor": lax.rem(tensor + step, PEERS)}, device_id_type=MESH
        )
        pl.semaphore_signal(
            barrier,
            inc=1,
            device_id={"section": lax.rem(section + step, SECTIONS)},
            device_id_type=MESH,
        )

    @pl.when(section == 0)
    def _():
        load_text.start()
        load_cotangent.start()

    dest = [dests[i] for i in range(SAMP)]
    offset = [offsets[i] for i in range(SAMP)]
    count = [counts[i] for i in range(SAMP)]

    row = iota((HALF - SAMP * SLOT, HALF), 0)
    table = jnp.where(row < SAMP, spread(row, offset), spread(row - SAMP, count))
    table = table.astype(F32).astype(BF16)
    place, lane = iota((DP * 16, HALF), 0), iota((DP * 16, HALF), 1)
    is_row = lane < SAMP * SLOT
    lane_sample = jnp.where(is_row, lax.shift_right_logical(lane, 3), lane & 7)
    lane_inner = jnp.where(is_row, lane & 7, lax.shift_right_logical(lane, 3))
    picks = (
        (lax.shift_right_logical(place, 4) == spread(lane_sample, dest))
        & ((place & 15) == lane_inner)
        & (lane < SAMP * SLOT + 2 * SAMP)
    )
    load_vision.wait()
    slots = jnp.dot(
        picks.astype(F32).astype(BF16),
        jnp.concatenate([vision_part[...], table], axis=0),
        preferred_element_type=F32,
    )
    outgoing[...] = slots.astype(BF16).reshape(DP, 16, HALF)
    arrived[me] = outgoing[me]
    load_weight.wait()
    load_gain.wait()

    @pl.when(section >= PLACERS)
    def _():
        load_proj.wait()

    pl.semaphore_wait(barrier, DP - 1 + 6)

    def send(ref, sent, arrival, device):
        pltpu.make_async_remote_copy(
            src_ref=ref,
            dst_ref=ref,
            send_sem=sent,
            recv_sem=arrival,
            device_id={"dp": device},
            device_id_type=MESH,
        ).start()

    def landed(ref, sent, arrival):
        pltpu.make_async_remote_copy(
            src_ref=ref,
            dst_ref=ref,
            send_sem=sent,
            recv_sem=arrival,
            device_id={"dp": near},
            device_id_type=MESH,
        ).wait_recv()

    def proj_block(slot):
        return proj_ring.at[slot]

    def weight_block(slot, cut):
        start = pl.multiple_of(slot * share_rows + cut[0], 16)
        return weight.at[pl.ds(start, cut[1])]

    def ring_start(block, arrival, sent, near_sem):
        for device in (right, left):
            send(block(me), sent, arrival(me), device)
        send(block(me), sent, near_sem, near)

    def ring_step(hop, block, arrival, sent, near_sem):
        from_left = lax.rem(chip + CHIPS - hop, CHIPS) * 2 + core
        from_right = lax.rem(chip + hop, CHIPS) * 2 + core
        if hop < CHIPS // 2:
            landed(block(from_left), sent, arrival(from_left))
            if hop < CHIPS // 2 - 1:
                send(block(from_left), sent, arrival(from_left), right)
            else:

                @pl.when(core == 0)
                def _():
                    send(block(from_left), sent, arrival(from_left), right)

            landed(block(from_right), sent, arrival(from_right))
            if hop < CHIPS // 2 - 1:
                send(block(from_right), sent, arrival(from_right), left)
            else:

                @pl.when(core == 1)
                def _():
                    send(block(from_right), sent, arrival(from_right), left)

            send(block(from_left), sent, near_sem, near)
            send(block(from_right), sent, near_sem, near)
        else:
            landed(block(from_left), sent, arrival(from_left))
            send(block(from_left), sent, near_sem, near)

    def weight_args(index):
        cut = WEIGHT_CUTS[index]
        return (
            lambda slot: weight_block(slot, cut),
            lambda slot: weight_sem.at[index, slot],
            weight_sent,
            weight_near,
        )

    def weight_step(hop):
        for index in range(len(WEIGHT_CUTS)):
            ring_step(hop, *weight_args(index))

    def proj_step(hop):
        ring_step(hop, *proj_args)

    proj_args = (proj_block, lambda slot: proj_sem.at[slot], proj_sent, proj_near)

    def scatter(source, target, sent, arrival):
        def one(step, carry):
            device = lax.rem(me + step, DP)
            pltpu.make_async_remote_copy(
                src_ref=source.at[device],
                dst_ref=target.at[me],
                send_sem=sent,
                recv_sem=arrival,
                device_id={"dp": device},
                device_id_type=MESH,
            ).start()
            return carry

        lax.fori_loop(1, DP, one, 0)

    def weight_start():
        for index in range(len(WEIGHT_CUTS)):
            ring_start(*weight_args(index))

    @pl.when(section >= PLACERS)
    def _():
        ring_start(*proj_args)

    @pl.when(section < PLACERS)
    def _():
        weight_start()

    scatter(outgoing, arrived, route_sent, route_sem)

    def of_sources():
        message = arrived[:, SLOT : SLOT + 2, :].astype(F32).astype(jnp.int32)
        return message[:, 0:1], message[:, 1:2]

    def gather_piece(step):
        return pltpu.make_async_remote_copy(
            src_ref=pieces.at[piece],
            dst_ref=pieces.at[piece],
            send_sem=pieces_sent.at[step - 1],
            recv_sem=pieces_sem.at[step - 1],
            device_id={"tensor": lax.rem(tensor + step, PEERS)},
            device_id_type=MESH,
        )

    def pack():
        wait_bytes(arrived.at[pl.ds(0, DP - 1)], route_sem)
        start_row, row_count = of_sources()
        shape = (DP, 16, HALF)
        inner, column = iota(shape, 1), iota(shape, 2)
        gathers = (
            (lax.shift_right_logical(start_row, 5) == lax.shift_right_logical(column, 3))
            & (inner == (column & 7))
            & (inner < row_count)
        )
        packed = lax.dot_general(
            gathers.astype(F32).astype(BF16).reshape(DP * 16, HALF),
            arrived[...].reshape(DP * 16, HALF),
            (((0,), (0,)), ((), ())),
            preferred_element_type=F32,
        )
        pieces[piece] = packed[: SAMP * SLOT].astype(BF16)
        for step in range(1, PEERS):
            gather_piece(step).start()

    def gather_rows(step):
        mine = pieces.at[pl.ds(section * PEERS, PEERS)]
        return pltpu.make_async_remote_copy(
            src_ref=mine,
            dst_ref=mine,
            send_sem=rows_sent.at[step - 1],
            recv_sem=rows_sem.at[step - 1],
            device_id={"section": lax.rem(section + step, SECTIONS)},
            device_id_type=MESH,
        )

    def pass_pieces():
        for step in range(1, PEERS):
            gather_piece(step).wait_recv()
        for step in range(1, SECTIONS):

            @pl.when(lax.rem(section + step, SECTIONS) >= PLACERS)
            def _():
                gather_rows(step).start()

    def hand_in(source):
        return pltpu.make_async_remote_copy(
            src_ref=images.at[source],
            dst_ref=images.at[source],
            send_sem=images_sent,
            recv_sem=images_sem.at[source],
            device_id={"section": 0},
            device_id_type=MESH,
        )

    def make_images():
        wait_bytes(proj_ring.at[pl.ds(0, CHIPS)], proj_near)
        for step in range(1, SECTIONS):
            gather_rows(step).wait_recv()
        image = jnp.dot(
            jnp.concatenate([pieces[index] for index in range(PIECES)], axis=1),
            proj_ring[...].reshape(DP * depth, FRONT),
            preferred_element_type=F32,
        )
        images[section] = image.astype(BF16)
        hand_in(section).start()

    def place_images():
        start_row, row_count = of_sources()
        start_row, row_count = start_row[:, 0], row_count[:, 0]
        mark = iota((DP, HALF), 1)
        of_doc = lax.shift_right_logical(start_row, 5) == lax.shift_right_logical(mark, 3)
        doc_row = jnp.sum(jnp.where(of_doc, start_row, 0), axis=0, keepdims=True)
        doc_count = jnp.sum(jnp.where(of_doc, row_count, 0), axis=0, keepdims=True)
        rows, mark = iota((text.shape[0], HALF), 0), iota((text.shape[0], HALF), 1)
        puts = (rows == doc_row + (mark & 7)) & ((mark & 7) < doc_count) & (mark < SAMP * SLOT)
        puts = puts.astype(F32)
        taken = jnp.sum(puts, axis=1, keepdims=True) > 0.0
        puts = puts[:, : SAMP * SLOT].astype(BF16)
        load_text.wait()
        for source in range(PLACERS, SECTIONS):
            hand_in(source).wait_recv()
        for tile, (source, part) in enumerate(IMAGE_TILES):
            columns = slice(tile * HALF, (tile + 1) * HALF)
            placed = jnp.dot(
                puts,
                images[source, :, part * HALF : (part + 1) * HALF],
                preferred_element_type=F32,
            )
            hidden[:, columns] = jnp.where(
                taken, placed, hidden[:, columns].astype(F32)
            ).astype(BF16)

    def send_back():
        load_cotangent.wait()
        start_row, row_count = of_sources()
        total = text.shape[0]
        start_row = jnp.concatenate([start_row] * (total // HALF), axis=2)
        row_count = jnp.concatenate([row_count] * (total // HALF), axis=2)
        shape = (DP, SLOT, total)
        inner, row = iota(shape, 1), iota(shape, 2)
        takes = (start_row + inner == row) & (inner < row_count)
        rows = jnp.dot(
            takes.astype(F32).reshape(DP * SLOT, total).astype(BF16),
            cotangent[...],
            preferred_element_type=F32,
        ).reshape(DP, SLOT, width)
        tiles = [rows[:, :, first : first + HALF] for first in range(0, width, HALF)]
        spare = jnp.zeros((DP, FOLDED - SLOT * len(tiles), HALF), F32)
        returning[...] = jnp.concatenate(tiles + [spare], axis=1).astype(BF16)
        back[me] = returning[me]
        scatter(returning, back, back_sent, back_sem)

    def exchange(step):
        return pltpu.make_async_remote_copy(
            src_ref=image_grad,
            dst_ref=image_grad,
            send_sem=grads_sent.at[step - 1],
            recv_sem=grads_sem,
            device_id={"section": step},
            device_id_type=MESH,
        )

    def collect():
        wait_bytes(back.at[pl.ds(0, DP - 1)], back_sem)
        found = [back[dest[i]].astype(F32) for i in range(SAMP)]
        for tile in range(width // HALF):
            rows = [each[tile * SLOT : (tile + 1) * SLOT] for each in found]
            image_grad[:, tile * HALF : (tile + 1) * HALF] = jnp.concatenate(
                rows, axis=0
            ).astype(BF16)
        for step in range(1, SECTIONS):
            exchange(step).start()

    def rows_of(micro):
        return pl.ds(pl.multiple_of(micro * ROWS, ROWS), ROWS)

    def relay(micro):
        return pltpu.make_async_remote_copy(
            src_ref=out.at[rows_of(micro)],
            dst_ref=hidden.at[rows_of(micro)],
            send_sem=out_sent.at[micro],
            recv_sem=hidden_sem.at[micro],
            device_id={"section": following},
            device_id_type=MESH,
        )

    def share(micro, step):
        return pltpu.make_async_remote_copy(
            src_ref=mixed.at[tensor, rows_of(micro)],
            dst_ref=mixed.at[tensor, rows_of(micro)],
            send_sem=mixed_sent.at[micro, step - 1],
            recv_sem=mixed_sem.at[micro, step - 1],
            device_id={"tensor": lax.rem(tensor + step, PEERS)},
            device_id_type=MESH,
        )

    def mix(micro):
        mixed[tensor, rows_of(micro)] = attend(hidden[rows_of(micro)], gain[...])
        for step in (2, 1, 3):
            share(micro, step).start()

    def project(micro):
        total = hidden[rows_of(micro)].astype(F32)
        for step in (0, 1, 3, 2):
            if step > 0:
                share(micro, step).wait_recv()
            peer = lax.rem(tensor + PEERS - step, PEERS)
            total += jnp.dot(
                mixed[peer, rows_of(micro)],
                weight[pl.ds(pl.multiple_of(peer * width, HEAD), width)],
                preferred_element_type=F32,
            )
        out[rows_of(micro)] = total.astype(BF16)

        @pl.when(section < SECTIONS - 1)
        def _():
            relay(micro).start()

    def mix_some(first, last):
        def one(micro, carry):
            mix(micro)
            return carry

        lax.fori_loop(first, last, one, 0)

    @pl.when(section < PLACERS)
    def _():
        weight_step(1)
        weight_step(2)
        pack()
        weight_step(3)
        pass_pieces()
        for hop in range(4, 8):
            weight_step(hop)

    @pl.when(section == 0)
    def _():
        place_images()
        mix_some(0, micros // 2)

    @pl.when(section < PLACERS)
    def _():
        weight_step(8)

    @pl.when(section == 0)
    def _():
        mix_some(micros // 2, micros)

    @pl.when(section >= PLACERS)
    def _():
        def weight_early(hop, first):
            @pl.when(section == first)
            def _():
                if hop == 0:
                    weight_start()
                else:
                    weight_step(hop)

        proj_step(1)
        proj_step(2)
        proj_step(3)
        weight_early(0, 2)
        pack()
        proj_step(4)
        pass_pieces()
        proj_step(5)
        proj_step(6)
        weight_early(1, 2)
        proj_step(7)
        weight_early(0, 3)
        proj_step(8)
        weight_early(2, 2)
        make_images()
        weight_early(1, 3)
        weight_early(2, 3)
        for hop in range(3, 9):
            weight_step(hop)

    wait_bytes(weight.at[pl.ds(0, CHIPS * share_rows)], weight_near)

    def step(turn, carry):
        @pl.when((section > 0) & (turn < micros))
        def _():
            relay(turn).wait_recv()
            mix(turn)

        @pl.when(turn > 0)
        def _():
            project(turn - 1)

        return carry

    lax.fori_loop(0, micros + 1, step, 0)

    @pl.when(section == 0)
    def _():
        send_back()
        collect()
        wait_bytes(returning.at[pl.ds(0, DP - 1)], back_sent)
        for step in range(1, SECTIONS):
            exchange(step).wait_send()

    @pl.when(section > 0)
    def _():
        exchange(1).wait_recv()

    wait_bytes(weight.at[pl.ds(0, (DP - 1) * share_rows)], weight_sent)
    wait_bytes(arrived.at[pl.ds(0, DP - 1)], route_sent)

    @pl.when(section >= PLACERS)
    def _():
        wait_bytes(proj_ring.at[pl.ds(0, DP - 1)], proj_sent)
        hand_in(section).wait_send()

    for step in range(1, PEERS):
        gather_piece(step).wait_send()
    for step in range(1, SECTIONS):

        @pl.when(lax.rem(section + step, SECTIONS) >= PLACERS)
        def _():
            gather_rows(step).wait_send()

    def drain(micro, carry):
        for step in range(1, PEERS):
            share(micro, step).wait_send()

        @pl.when(section < SECTIONS - 1)
        def _():
            relay(micro).wait_send()

        return carry

    lax.fori_loop(0, micros, drain, 0)


def on_device(
    text_embed,
    vision,
    proj_weight,
    out_weight,
    qk_gain,
    image_counts,
    sample_shard,
    sample_offset,
    embed_grad,
):
    rows, width = text_embed.shape
    micros = rows // ROWS
    depth = proj_weight.shape[0]
    vmem = pl.BlockSpec(memory_space=pltpu.VMEM)
    hbm = pl.BlockSpec(memory_space=pl.ANY)
    smem = pl.BlockSpec(memory_space=pltpu.SMEM)
    dma = pltpu.SemaphoreType.DMA
    outputs, image_grad = pl.pallas_call(
        whole_kernel,
        out_shape=(
            jax.ShapeDtypeStruct((rows, width), BF16),
            jax.ShapeDtypeStruct((vision.shape[0], width), BF16),
        ),
        in_specs=[hbm] * 5 + [smem] * 3 + [hbm],
        out_specs=(vmem, vmem),
        scratch_shapes=[
            pltpu.VMEM((1, width), F32),
            pltpu.VMEM((vision.shape[0], HALF), BF16),
            pltpu.VMEM((rows, width), BF16),
            pltpu.VMEM((DP, depth, FRONT), BF16),
            pltpu.VMEM((DP * out_weight.shape[1], width), BF16),
            pltpu.VMEM((DP, 16, HALF), BF16),
            pltpu.VMEM((DP, 16, HALF), BF16),
            pltpu.VMEM((PIECES, SAMP * SLOT, HALF), BF16),
            pltpu.VMEM((SECTIONS, SAMP * SLOT, FRONT), BF16),
            pltpu.VMEM((DP, FOLDED, HALF), BF16),
            pltpu.VMEM((DP, FOLDED, HALF), BF16),
            pltpu.VMEM((rows, width), BF16),
            pltpu.VMEM((PEERS, rows, width), BF16),
            dma((6,)),
            dma((PEERS - 1,)),
            dma((PEERS - 1,)),
            dma((SECTIONS - 1,)),
            dma((SECTIONS - 1,)),
            dma((DP,)),
            dma,
            dma,
            dma((len(WEIGHT_CUTS), DP)),
            dma,
            dma,
            dma,
            dma,
            dma,
            dma,
            dma((SECTIONS,)),
            dma,
            dma,
            dma((SECTIONS - 1,)),
            dma((micros,)),
            dma((micros, PEERS - 1)),
            dma((micros,)),
            dma((micros, PEERS - 1)),
        ],
        compiler_params=pltpu.CompilerParams(
            collective_id=0, has_side_effects=True, vmem_limit_bytes=60 * 1024 * 1024
        ),
    )(
        text_embed,
        vision,
        proj_weight,
        out_weight[0],
        qk_gain,
        image_counts,
        sample_shard,
        sample_offset,
        embed_grad,
    )
    return (outputs[None], image_grad)


def solution(mesh):
    placed = (
        P("dp", "tensor"),
        P("dp", None),
        P("dp", "tensor"),
        P("section", "dp", "tensor"),
        P("section", "tensor"),
        P("dp"),
        P("dp"),
        P("dp"),
        P("dp", "tensor"),
    )
    return jax.shard_map(
        on_device,
        mesh=mesh,
        in_specs=placed,
        out_specs=(P("section", "dp", "tensor"), P("dp", "tensor")),
        check_vma=False,
    )
```

```python
import jax
import jax.numpy as jnp
from jax import lax
from jax.experimental import pallas as pl
from jax.experimental.pallas import tpu as pltpu
from jax.sharding import PartitionSpec as P

HEAD = 128
DOC = 32
SLOT = 8
SAMP = 8
ROWS = 32
SECTIONS = 4
PEERS = 4
DP = 32
CHIPS = 16
PIECES = 16
HALF = 128
FRONT = 512
FOLDED = 64
BACK_TURN = 4
PLACERS = 2
WEIGHT_CUTS = ((0, 64), (64, 48))
IMAGE_TILES = ((2, 0), (2, 1), (2, 2), (2, 3), (3, 1), (3, 2), (3, 3))
TILES = ((1, 0), (1, 1), (2, 0), (2, 1), (3, 0), (3, 1), (3, 2))
MESH = pl.DeviceIdType.MESH
BF16 = jnp.bfloat16
F32 = jnp.float32


def attend(x, gains):
    rows = x.shape[0]
    row, col = iota((rows, rows), 0), iota((rows, rows), 1)
    allowed = (col <= row) & (lax.div(col, DOC) == lax.div(row, DOC))
    cuts = [slice(first, first + HEAD) for first in range(0, x.shape[1], HEAD)]
    values = [x[:, cut] for cut in cuts]
    wide = [value.astype(F32) for value in values]
    means = [jnp.mean(value * value, axis=-1, keepdims=True) for value in wide]
    normed = [
        (value * lax.rsqrt(mean + 1e-06) * gains[:, cut]).astype(BF16)
        for value, mean, cut in zip(wide, means, cuts)
    ]
    scores = [
        lax.dot_general(each, each, (((1,), (1,)), ((), ())), preferred_element_type=F32)
        for each in normed
    ]
    weights = [jnp.where(allowed, jnp.exp(score * (2.0 / HEAD)), 0.0) for score in scores]
    weights = [(each / jnp.sum(each, axis=-1, keepdims=True)).astype(BF16) for each in weights]
    mixed = [
        jnp.dot(each, value, preferred_element_type=F32).astype(BF16)
        for each, value in zip(weights, values)
    ]
    return jnp.concatenate(mixed, axis=1)


def iota(shape, dim):
    return lax.broadcasted_iota(jnp.int32, shape, dim)


def spread(index, scalars):
    total = jnp.zeros(index.shape, jnp.int32)
    for i in range(SAMP):
        total = jnp.where(index == i, scalars[i], total)
    return total


def wait_bytes(ref, sem):
    pltpu.make_async_copy(ref, ref, sem).wait()


def whole_kernel(
    text,
    vision,
    proj,
    shard_weight,
    gain_input,
    counts,
    dests,
    offsets,
    cotangent_input,
    out,
    image_grad,
    gain,
    vision_part,
    cotangent,
    proj_ring,
    weight,
    outgoing,
    arrived,
    pieces,
    images,
    returning,
    back,
    hidden,
    mixed,
    load_sem,
    pieces_sem,
    pieces_sent,
    rows_sem,
    rows_sent,
    proj_sem,
    proj_sent,
    weight_sem,
    weight_near,
    weight_sent,
    route_sem,
    route_sent,
    back_sem,
    back_sent,
    images_sem,
    images_sent,
    grads_sem,
    grads_sent,
    hidden_sem,
    mixed_sem,
    out_sent,
    mixed_sent,
):
    section, tensor = lax.axis_index("section"), lax.axis_index("tensor")
    me = lax.axis_index("dp")
    chip, core = lax.div(me, 2), lax.rem(me, 2)
    width = hidden.shape[1]
    micros = hidden.shape[0] // ROWS
    following = lax.rem(section + 1, SECTIONS)
    right = lax.rem(chip + 1, CHIPS) * 2 + core
    left = lax.rem(chip + CHIPS - 1, CHIPS) * 2 + core
    near = chip * 2 + 1 - core
    image_column = pl.multiple_of(lax.div(section, 3) * 3 * HALF, HALF)
    piece = section * PEERS + tensor
    depth, share_rows = proj.shape[0], shard_weight.shape[0]

    def load(source, target, index):
        return pltpu.make_async_copy(source, target, load_sem.at[index])

    own = pl.multiple_of(me * share_rows, 16)
    load_weight = load(shard_weight, weight.at[pl.ds(own, share_rows)], 0)
    load_vision = load(
        vision.at[:, pl.ds(pl.multiple_of(piece * HALF, HALF), HALF)], vision_part, 1
    )
    load_cotangent = load(cotangent_input, cotangent, 2)
    load_text = load(text, hidden, 3)
    load_proj = load(proj.at[:, pl.ds(image_column, FRONT)], proj_ring.at[me], 4)
    load_gain = load(gain_input, gain, 5)
    load_weight.start()
    load_gain.start()
    load_vision.start()

    @pl.when(section >= PLACERS)
    def _():
        load_proj.start()

    barrier = pltpu.get_barrier_semaphore()

    def greet(step, carry):
        pl.semaphore_signal(
            barrier, inc=1, device_id={"dp": lax.rem(me + step, DP)}, device_id_type=MESH
        )
        return carry

    lax.fori_loop(1, DP, greet, 0)
    for step in range(1, 4):
        pl.semaphore_signal(
            barrier, inc=1, device_id={"tensor": lax.rem(tensor + step, PEERS)}, device_id_type=MESH
        )
        pl.semaphore_signal(
            barrier,
            inc=1,
            device_id={"section": lax.rem(section + step, SECTIONS)},
            device_id_type=MESH,
        )

    @pl.when(section == 0)
    def _():
        load_text.start()
        load_cotangent.start()

    dest = [dests[i] for i in range(SAMP)]
    offset = [offsets[i] for i in range(SAMP)]
    count = [counts[i] for i in range(SAMP)]

    load_weight.wait()

    @pl.when(section >= PLACERS)
    def _():
        load_proj.wait()

    pl.semaphore_wait(barrier, DP - 1 + 6)

    def send(ref, sent, arrival, device):
        pltpu.make_async_remote_copy(
            src_ref=ref,
            dst_ref=ref,
            send_sem=sent,
            recv_sem=arrival,
            device_id={"dp": device},
            device_id_type=MESH,
        ).start()

    def landed(ref, sent, arrival):
        pltpu.make_async_remote_copy(
            src_ref=ref,
            dst_ref=ref,
            send_sem=sent,
            recv_sem=arrival,
            device_id={"dp": near},
            device_id_type=MESH,
        ).wait_recv()

    def proj_block(slot):
        return proj_ring.at[slot]

    def weight_block(slot, cut):
        start = pl.multiple_of(slot * share_rows + cut[0], 16)
        return weight.at[pl.ds(start, cut[1])]

    def ring_start(block, arrival, sent, near_at):
        for device in (right, left):
            send(block(me), sent, arrival(me), device)
        send(block(me), sent, near_at(me), near)

    def ring_step(hop, block, arrival, sent, near_at):
        from_left = lax.rem(chip + CHIPS - hop, CHIPS) * 2 + core
        from_right = lax.rem(chip + hop, CHIPS) * 2 + core
        if hop < CHIPS // 2:
            landed(block(from_left), sent, arrival(from_left))
            if hop < CHIPS // 2 - 1:
                send(block(from_left), sent, arrival(from_left), right)
            else:

                @pl.when(core == 0)
                def _():
                    send(block(from_left), sent, arrival(from_left), right)

            landed(block(from_right), sent, arrival(from_right))
            if hop < CHIPS // 2 - 1:
                send(block(from_right), sent, arrival(from_right), left)
            else:

                @pl.when(core == 1)
                def _():
                    send(block(from_right), sent, arrival(from_right), left)

            send(block(from_left), sent, near_at(from_left), near)
            send(block(from_right), sent, near_at(from_right), near)
        else:
            landed(block(from_left), sent, arrival(from_left))
            send(block(from_left), sent, near_at(from_left), near)

    def weight_args(index):
        cut = WEIGHT_CUTS[index]
        return (
            lambda slot: weight_block(slot, cut),
            lambda slot: weight_sem.at[index, slot],
            weight_sent,
            lambda slot: weight_near,
        )

    def weight_step(hop):
        for index in range(len(WEIGHT_CUTS)):
            ring_step(hop, *weight_args(index))

    def proj_step(hop):
        ring_step(hop, *proj_args)

    def proj_arrival(slot):
        return proj_sem.at[slot]

    proj_args = (proj_block, proj_arrival, proj_sent, proj_arrival)

    def scatter(source, target, sent, arrival):
        def one(step, carry):
            device = lax.rem(me + step, DP)
            pltpu.make_async_remote_copy(
                src_ref=source.at[device],
                dst_ref=target.at[me],
                send_sem=sent,
                recv_sem=arrival,
                device_id={"dp": device},
                device_id_type=MESH,
            ).start()
            return carry

        lax.fori_loop(1, DP, one, 0)

    def weight_start():
        for index in range(len(WEIGHT_CUTS)):
            ring_start(*weight_args(index))

    @pl.when(section >= PLACERS)
    def _():
        ring_start(*proj_args)

    @pl.when(section < PLACERS)
    def _():
        weight_start()

    row = iota((HALF - SAMP * SLOT, HALF), 0)
    table = jnp.where(row < SAMP, spread(row, offset), spread(row - SAMP, count))
    table = table.astype(F32).astype(BF16)
    place, lane = iota((DP * 16, HALF), 0), iota((DP * 16, HALF), 1)
    is_row = lane < SAMP * SLOT
    lane_sample = jnp.where(is_row, lax.shift_right_logical(lane, 3), lane & 7)
    lane_inner = jnp.where(is_row, lane & 7, lax.shift_right_logical(lane, 3))
    picks = (
        (lax.shift_right_logical(place, 4) == spread(lane_sample, dest))
        & ((place & 15) == lane_inner)
        & (lane < SAMP * SLOT + 2 * SAMP)
    )
    load_vision.wait()
    slots = jnp.dot(
        picks.astype(F32).astype(BF16),
        jnp.concatenate([vision_part[...], table], axis=0),
        preferred_element_type=F32,
    )
    outgoing[...] = slots.astype(BF16).reshape(DP, 16, HALF)
    arrived[me] = outgoing[me]
    scatter(outgoing, arrived, route_sent, route_sem)
    load_gain.wait()

    def of_sources():
        message = arrived[:, SLOT : SLOT + 2, :].astype(F32).astype(jnp.int32)
        return message[:, 0:1], message[:, 1:2]

    def gather_piece(step):
        return pltpu.make_async_remote_copy(
            src_ref=pieces.at[piece],
            dst_ref=pieces.at[piece],
            send_sem=pieces_sent.at[step - 1],
            recv_sem=pieces_sem.at[step - 1],
            device_id={"tensor": lax.rem(tensor + step, PEERS)},
            device_id_type=MESH,
        )

    def pack():
        wait_bytes(arrived.at[pl.ds(0, DP - 1)], route_sem)
        start_row, row_count = of_sources()
        shape = (DP, 16, HALF)
        inner, column = iota(shape, 1), iota(shape, 2)
        gathers = (
            (lax.shift_right_logical(start_row, 5) == lax.shift_right_logical(column, 3))
            & (inner == (column & 7))
            & (inner < row_count)
        )
        packed = lax.dot_general(
            gathers.astype(F32).astype(BF16).reshape(DP * 16, HALF),
            arrived[...].reshape(DP * 16, HALF),
            (((0,), (0,)), ((), ())),
            preferred_element_type=F32,
        )
        pieces[piece] = packed[: SAMP * SLOT].astype(BF16)
        for step in range(1, PEERS):
            gather_piece(step).start()

    def gather_rows(step):
        mine = pieces.at[pl.ds(section * PEERS, PEERS)]
        return pltpu.make_async_remote_copy(
            src_ref=mine,
            dst_ref=mine,
            send_sem=rows_sent.at[step - 1],
            recv_sem=rows_sem.at[step - 1],
            device_id={"section": lax.rem(section + step, SECTIONS)},
            device_id_type=MESH,
        )

    def pass_pieces():
        for step in range(1, PEERS):
            gather_piece(step).wait_recv()
        for step in range(1, SECTIONS):

            @pl.when(lax.rem(section + step, SECTIONS) >= PLACERS)
            def _():
                gather_rows(step).start()

    def hand_in(source):
        return pltpu.make_async_remote_copy(
            src_ref=images.at[source],
            dst_ref=images.at[source],
            send_sem=images_sent,
            recv_sem=images_sem.at[source],
            device_id={"section": 0},
            device_id_type=MESH,
        )

    def times_columns(offsets):
        total = None
        for step in offsets:
            there = lax.rem(chip + CHIPS + step, CHIPS)
            other = there * 2 + 1 - core
            landed(proj_block(other), proj_sent, proj_arrival(other))
            term = jnp.dot(
                pieces[there],
                proj_ring[pl.ds(there * 2, 2)].reshape(2 * depth, FRONT),
                preferred_element_type=F32,
            )
            total = term if total is None else total + term
        return total

    def doc_tables():
        start_row, row_count = of_sources()
        start_row, row_count = start_row[:, 0], row_count[:, 0]
        mark = iota((DP, HALF), 1)
        of_doc = lax.shift_right_logical(start_row, 5) == lax.shift_right_logical(mark, 3)
        doc_row = jnp.sum(jnp.where(of_doc, start_row, 0), axis=0, keepdims=True)
        doc_count = jnp.sum(jnp.where(of_doc, row_count, 0), axis=0, keepdims=True)
        return doc_row, doc_count

    def place(micro, doc_row, doc_count):
        row, mark = iota((ROWS, HALF), 0) + micro * ROWS, iota((ROWS, HALF), 1)
        puts = (row == doc_row + (mark & 7)) & ((mark & 7) < doc_count) & (mark < SAMP * SLOT)
        puts = puts.astype(F32)
        taken = jnp.sum(puts, axis=1, keepdims=True) > 0.0
        puts = puts[:, : SAMP * SLOT].astype(BF16)
        here = pl.ds(pl.multiple_of(micro * ROWS, ROWS), ROWS)
        placed = [
            jnp.dot(
                puts,
                images[source, :, part * HALF : (part + 1) * HALF],
                preferred_element_type=F32,
            )
            for source, part in IMAGE_TILES
        ]
        placed = jnp.concatenate(placed, axis=1)
        hidden[here] = jnp.where(taken, placed, hidden[here].astype(F32)).astype(BF16)

    def prepare_back():
        load_cotangent.wait()
        start_row, row_count = of_sources()
        total = text.shape[0]
        start_row = jnp.concatenate([start_row] * (total // HALF), axis=2)
        row_count = jnp.concatenate([row_count] * (total // HALF), axis=2)
        shape = (DP, SLOT, total)
        inner, row = iota(shape, 1), iota(shape, 2)
        takes = (start_row + inner == row) & (inner < row_count)
        rows = jnp.dot(
            takes.astype(F32).reshape(DP * SLOT, total).astype(BF16),
            cotangent[...],
            preferred_element_type=F32,
        ).reshape(DP, SLOT, width)
        tiles = [rows[:, :, first : first + HALF] for first in range(0, width, HALF)]
        spare = jnp.zeros((DP, FOLDED - SLOT * len(tiles), HALF), F32)
        returning[...] = jnp.concatenate(tiles + [spare], axis=1).astype(BF16)
        back[me] = returning[me]

    def exchange(step):
        return pltpu.make_async_remote_copy(
            src_ref=image_grad,
            dst_ref=image_grad,
            send_sem=grads_sent.at[step - 1],
            recv_sem=grads_sem,
            device_id={"section": step},
            device_id_type=MESH,
        )

    def collect():
        wait_bytes(back.at[pl.ds(0, DP - 1)], back_sem)
        found = [back[dest[i]].astype(F32) for i in range(SAMP)]
        for tile in range(width // HALF):
            rows = [each[tile * SLOT : (tile + 1) * SLOT] for each in found]
            image_grad[:, tile * HALF : (tile + 1) * HALF] = jnp.concatenate(
                rows, axis=0
            ).astype(BF16)
        for step in range(1, SECTIONS):
            exchange(step).start()

    def rows_of(micro):
        return pl.ds(pl.multiple_of(micro * ROWS, ROWS), ROWS)

    def relay(micro):
        return pltpu.make_async_remote_copy(
            src_ref=out.at[rows_of(micro)],
            dst_ref=hidden.at[rows_of(micro)],
            send_sem=out_sent.at[micro],
            recv_sem=hidden_sem.at[micro],
            device_id={"section": following},
            device_id_type=MESH,
        )

    def share(micro, step):
        return pltpu.make_async_remote_copy(
            src_ref=mixed.at[tensor, rows_of(micro)],
            dst_ref=mixed.at[tensor, rows_of(micro)],
            send_sem=mixed_sent.at[micro, step - 1],
            recv_sem=mixed_sem.at[micro, step - 1],
            device_id={"tensor": lax.rem(tensor + step, PEERS)},
            device_id_type=MESH,
        )

    def mix(micro):
        mixed[tensor, rows_of(micro)] = attend(hidden[rows_of(micro)], gain[...])
        for step in (2, 1, 3):
            share(micro, step).start()

    def project(micro):
        total = hidden[rows_of(micro)].astype(F32)
        for step in (0, 1, 3, 2):
            if step > 0:
                share(micro, step).wait_recv()
            peer = lax.rem(tensor + PEERS - step, PEERS)
            total += jnp.dot(
                mixed[peer, rows_of(micro)],
                weight[pl.ds(pl.multiple_of(peer * width, HEAD), width)],
                preferred_element_type=F32,
            )
        out[rows_of(micro)] = total.astype(BF16)

        @pl.when(section < SECTIONS - 1)
        def _():
            relay(micro).start()

    def mix_some(first, last):
        doc_row, doc_count = doc_tables()

        def one(micro, carry):
            place(micro, doc_row, doc_count)
            mix(micro)
            return carry

        lax.fori_loop(first, last, one, 0)

    @pl.when(section < PLACERS)
    def _():
        weight_step(1)
        weight_step(2)
        pack()
        weight_step(3)
        pass_pieces()
        weight_step(4)

        @pl.when(section == 0)
        def _():
            prepare_back()

        for hop in range(5, 8):
            weight_step(hop)

    @pl.when(section == 0)
    def _():
        load_text.wait()
        for source in range(PLACERS, SECTIONS):
            hand_in(source).wait_recv()
        mix_some(0, micros // 2)

    @pl.when(section < PLACERS)
    def _():
        weight_step(8)

    @pl.when(section == 0)
    def _():
        mix_some(micros // 2, micros)

    @pl.when(section >= PLACERS)
    def _():
        def weight_early(hop, first):
            @pl.when(section == first)
            def _():
                if hop == 0:
                    weight_start()
                else:
                    weight_step(hop)

        def weight_early(hop, first):
            @pl.when(section == first)
            def _():
                if hop == 0:
                    weight_start()
                else:
                    weight_step(hop)

        proj_step(1)
        weight_early(0, 2)
        weight_early(0, 3)
        proj_step(2)
        proj_step(3)
        pack()
        proj_step(4)
        weight_early(1, 2)
        weight_early(1, 3)
        pass_pieces()
        proj_step(5)
        proj_step(6)
        weight_early(2, 2)
        weight_early(2, 3)
        for step in range(1, SECTIONS):
            gather_rows(step).wait_recv()
        total = times_columns((0, 1, -1, 2, -2, 3, -3, 4, -4, 5, -5))
        proj_step(7)
        total += times_columns((6, -6))
        proj_step(8)
        weight_early(3, 2)
        weight_early(3, 3)
        total += times_columns((7, -7, 8))
        images[section] = total.astype(BF16)
        hand_in(section).start()
        for hop in range(4, 9):
            weight_step(hop)

    wait_bytes(weight.at[pl.ds(0, CHIPS * share_rows)], weight_near)

    def step(turn, carry):
        @pl.when((section > 0) & (turn < micros))
        def _():
            relay(turn).wait_recv()
            mix(turn)

        @pl.when(turn > 1)
        def _():
            project(turn - 2)

        @pl.when((section == 0) & (turn == BACK_TURN))
        def _():
            scatter(returning, back, back_sent, back_sem)

        return carry

    lax.fori_loop(0, micros + 2, step, 0)

    @pl.when(section == 0)
    def _():
        collect()
        wait_bytes(returning.at[pl.ds(0, DP - 1)], back_sent)
        for step in range(1, SECTIONS):
            exchange(step).wait_send()

    @pl.when(section > 0)
    def _():
        exchange(1).wait_recv()

    wait_bytes(weight.at[pl.ds(0, (DP - 1) * share_rows)], weight_sent)
    wait_bytes(arrived.at[pl.ds(0, DP - 1)], route_sent)

    @pl.when(section >= PLACERS)
    def _():
        wait_bytes(proj_ring.at[pl.ds(0, DP - 1)], proj_sent)
        hand_in(section).wait_send()

    for step in range(1, PEERS):
        gather_piece(step).wait_send()
    for step in range(1, SECTIONS):

        @pl.when(lax.rem(section + step, SECTIONS) >= PLACERS)
        def _():
            gather_rows(step).wait_send()

    def drain(micro, carry):
        for step in range(1, PEERS):
            share(micro, step).wait_send()

        @pl.when(section < SECTIONS - 1)
        def _():
            relay(micro).wait_send()

        return carry

    lax.fori_loop(0, micros, drain, 0)


def on_device(
    text_embed,
    vision,
    proj_weight,
    out_weight,
    qk_gain,
    image_counts,
    sample_shard,
    sample_offset,
    embed_grad,
):
    rows, width = text_embed.shape
    micros = rows // ROWS
    depth = proj_weight.shape[0]
    vmem = pl.BlockSpec(memory_space=pltpu.VMEM)
    hbm = pl.BlockSpec(memory_space=pl.ANY)
    smem = pl.BlockSpec(memory_space=pltpu.SMEM)
    dma = pltpu.SemaphoreType.DMA
    outputs, image_grad = pl.pallas_call(
        whole_kernel,
        out_shape=(
            jax.ShapeDtypeStruct((rows, width), BF16),
            jax.ShapeDtypeStruct((vision.shape[0], width), BF16),
        ),
        in_specs=[hbm] * 5 + [smem] * 3 + [hbm],
        out_specs=(vmem, vmem),
        scratch_shapes=[
            pltpu.VMEM((1, width), F32),
            pltpu.VMEM((vision.shape[0], HALF), BF16),
            pltpu.VMEM((rows, width), BF16),
            pltpu.VMEM((DP, depth, FRONT), BF16),
            pltpu.VMEM((DP * out_weight.shape[1], width), BF16),
            pltpu.VMEM((DP, 16, HALF), BF16),
            pltpu.VMEM((DP, 16, HALF), BF16),
            pltpu.VMEM((PIECES, SAMP * SLOT, HALF), BF16),
            pltpu.VMEM((SECTIONS, SAMP * SLOT, FRONT), BF16),
            pltpu.VMEM((DP, FOLDED, HALF), BF16),
            pltpu.VMEM((DP, FOLDED, HALF), BF16),
            pltpu.VMEM((rows, width), BF16),
            pltpu.VMEM((PEERS, rows, width), BF16),
            dma((6,)),
            dma((PEERS - 1,)),
            dma((PEERS - 1,)),
            dma((SECTIONS - 1,)),
            dma((SECTIONS - 1,)),
            dma((DP,)),
            dma,
            dma((len(WEIGHT_CUTS), DP)),
            dma,
            dma,
            dma,
            dma,
            dma,
            dma,
            dma((SECTIONS,)),
            dma,
            dma,
            dma((SECTIONS - 1,)),
            dma((micros,)),
            dma((micros, PEERS - 1)),
            dma((micros,)),
            dma((micros, PEERS - 1)),
        ],
        compiler_params=pltpu.CompilerParams(
            collective_id=0, has_side_effects=True, vmem_limit_bytes=60 * 1024 * 1024
        ),
    )(
        text_embed,
        vision,
        proj_weight,
        out_weight[0],
        qk_gain,
        image_counts,
        sample_shard,
        sample_offset,
        embed_grad,
    )
    return (outputs[None], image_grad)


def solution(mesh):
    placed = (
        P("dp", "tensor"),
        P("dp", None),
        P("dp", "tensor"),
        P("section", "dp", "tensor"),
        P("section", "tensor"),
        P("dp"),
        P("dp"),
        P("dp"),
        P("dp", "tensor"),
    )
    return jax.shard_map(
        on_device,
        mesh=mesh,
        in_specs=placed,
        out_specs=(P("section", "dp", "tensor"), P("dp", "tensor")),
        check_vma=False,
    )
```

```python
import jax
import jax.numpy as jnp
from jax import lax
from jax.experimental import pallas as pl
from jax.experimental.pallas import tpu as pltpu
from jax.sharding import PartitionSpec as P

HEAD = 128
DOC = 32
SLOT = 8
SAMP = 8
ROWS = 32
SECTIONS = 4
PEERS = 4
DP = 32
CHIPS = 16
PIECES = 16
HALF = 128
FRONT = 512
FOLDED = 64
BACK_TURN = 4
PLACERS = 2
WEIGHT_CUTS = ((0, 64), (64, 48))
IMAGE_TILES = ((2, 0), (2, 1), (2, 2), (2, 3), (3, 1), (3, 2), (3, 3))
TILES = ((1, 0), (1, 1), (2, 0), (2, 1), (3, 0), (3, 1), (3, 2))
MESH = pl.DeviceIdType.MESH
BF16 = jnp.bfloat16
F32 = jnp.float32


def attend(x, gains):
    rows = x.shape[0]
    row, col = iota((rows, rows), 0), iota((rows, rows), 1)
    allowed = (col <= row) & (lax.div(col, DOC) == lax.div(row, DOC))
    cuts = [slice(first, first + HEAD) for first in range(0, x.shape[1], HEAD)]
    values = [x[:, cut] for cut in cuts]
    wide = [value.astype(F32) for value in values]
    means = [jnp.mean(value * value, axis=-1, keepdims=True) for value in wide]
    normed = [
        (value * lax.rsqrt(mean + 1e-06) * gains[:, cut]).astype(BF16)
        for value, mean, cut in zip(wide, means, cuts)
    ]
    scores = [
        lax.dot_general(each, each, (((1,), (1,)), ((), ())), preferred_element_type=F32)
        for each in normed
    ]
    weights = [jnp.where(allowed, jnp.exp(score * (2.0 / HEAD)), 0.0) for score in scores]
    weights = [(each / jnp.sum(each, axis=-1, keepdims=True)).astype(BF16) for each in weights]
    mixed = [
        jnp.dot(each, value, preferred_element_type=F32).astype(BF16)
        for each, value in zip(weights, values)
    ]
    return jnp.concatenate(mixed, axis=1)


def iota(shape, dim):
    return lax.broadcasted_iota(jnp.int32, shape, dim)


def spread(index, scalars):
    total = jnp.zeros(index.shape, jnp.int32)
    for i in range(SAMP):
        total = jnp.where(index == i, scalars[i], total)
    return total


def wait_bytes(ref, sem):
    pltpu.make_async_copy(ref, ref, sem).wait()


def whole_kernel(
    text,
    vision,
    proj,
    shard_weight,
    gain_input,
    counts,
    dests,
    offsets,
    cotangent_input,
    out_result,
    image_grad_result,
    out,
    image_grad,
    gain,
    vision_part,
    cotangent,
    proj_ring,
    weight,
    outgoing,
    arrived,
    pieces,
    images,
    returning,
    back,
    hidden,
    mixed,
    load_sem,
    store_sem,
    store_grad_sem,
    pieces_sem,
    pieces_sent,
    rows_sem,
    rows_sent,
    proj_sem,
    proj_sent,
    weight_sem,
    weight_near,
    weight_sent,
    route_sem,
    route_sent,
    back_sem,
    back_sent,
    images_sem,
    images_sent,
    grads_sem,
    grads_sent,
    hidden_sem,
    mixed_sem,
    out_sent,
    mixed_sent,
):
    section, tensor = lax.axis_index("section"), lax.axis_index("tensor")
    me = lax.axis_index("dp")
    chip, core = lax.div(me, 2), lax.rem(me, 2)
    width = hidden.shape[1]
    micros = hidden.shape[0] // ROWS
    following = lax.rem(section + 1, SECTIONS)
    right = lax.rem(chip + 1, CHIPS) * 2 + core
    left = lax.rem(chip + CHIPS - 1, CHIPS) * 2 + core
    near = chip * 2 + 1 - core
    image_column = pl.multiple_of(lax.div(section, 3) * 3 * HALF, HALF)
    piece = section * PEERS + tensor
    depth, share_rows = proj.shape[0], shard_weight.shape[0]

    def load(source, target, index):
        return pltpu.make_async_copy(source, target, load_sem.at[index])

    own = pl.multiple_of(me * share_rows, 16)
    load_weight = load(shard_weight, weight.at[pl.ds(own, share_rows)], 0)
    load_vision = load(
        vision.at[:, pl.ds(pl.multiple_of(piece * HALF, HALF), HALF)], vision_part, 1
    )
    load_cotangent = load(cotangent_input, cotangent, 2)
    load_text = load(text, hidden, 3)
    load_proj = load(proj.at[:, pl.ds(image_column, FRONT)], proj_ring.at[me], 4)
    load_gain = load(gain_input, gain, 5)
    load_weight.start()
    load_gain.start()
    load_vision.start()

    @pl.when(section >= PLACERS)
    def _():
        load_proj.start()

    barrier = pltpu.get_barrier_semaphore()

    def greet(step, carry):
        pl.semaphore_signal(
            barrier, inc=1, device_id={"dp": lax.rem(me + step, DP)}, device_id_type=MESH
        )
        return carry

    lax.fori_loop(1, DP, greet, 0)
    for step in range(1, 4):
        pl.semaphore_signal(
            barrier, inc=1, device_id={"tensor": lax.rem(tensor + step, PEERS)}, device_id_type=MESH
        )
        pl.semaphore_signal(
            barrier,
            inc=1,
            device_id={"section": lax.rem(section + step, SECTIONS)},
            device_id_type=MESH,
        )

    @pl.when(section == 0)
    def _():
        load_text.start()
        load_cotangent.start()

    dest = [dests[i] for i in range(SAMP)]
    offset = [offsets[i] for i in range(SAMP)]
    count = [counts[i] for i in range(SAMP)]

    load_weight.wait()

    @pl.when(section >= PLACERS)
    def _():
        load_proj.wait()

    pl.semaphore_wait(barrier, DP - 1 + 6)

    def send(ref, sent, arrival, device):
        pltpu.make_async_remote_copy(
            src_ref=ref,
            dst_ref=ref,
            send_sem=sent,
            recv_sem=arrival,
            device_id={"dp": device},
            device_id_type=MESH,
        ).start()

    def landed(ref, sent, arrival):
        pltpu.make_async_remote_copy(
            src_ref=ref,
            dst_ref=ref,
            send_sem=sent,
            recv_sem=arrival,
            device_id={"dp": near},
            device_id_type=MESH,
        ).wait_recv()

    def proj_block(slot):
        return proj_ring.at[slot]

    def weight_block(slot, cut):
        start = pl.multiple_of(slot * share_rows + cut[0], 16)
        return weight.at[pl.ds(start, cut[1])]

    def ring_start(block, arrival, sent, near_at):
        for device in (right, left):
            send(block(me), sent, arrival(me), device)
        send(block(me), sent, near_at(me), near)

    def ring_step(hop, block, arrival, sent, near_at):
        from_left = lax.rem(chip + CHIPS - hop, CHIPS) * 2 + core
        from_right = lax.rem(chip + hop, CHIPS) * 2 + core
        if hop < CHIPS // 2:
            landed(block(from_left), sent, arrival(from_left))
            if hop < CHIPS // 2 - 1:
                send(block(from_left), sent, arrival(from_left), right)
            else:

                @pl.when(core == 0)
                def _():
                    send(block(from_left), sent, arrival(from_left), right)

            landed(block(from_right), sent, arrival(from_right))
            if hop < CHIPS // 2 - 1:
                send(block(from_right), sent, arrival(from_right), left)
            else:

                @pl.when(core == 1)
                def _():
                    send(block(from_right), sent, arrival(from_right), left)

            send(block(from_left), sent, near_at(from_left), near)
            send(block(from_right), sent, near_at(from_right), near)
        else:
            landed(block(from_left), sent, arrival(from_left))
            send(block(from_left), sent, near_at(from_left), near)

    def weight_args(index):
        cut = WEIGHT_CUTS[index]
        return (
            lambda slot: weight_block(slot, cut),
            lambda slot: weight_sem.at[index, slot],
            weight_sent,
            lambda slot: weight_near,
        )

    def weight_step(hop):
        for index in range(len(WEIGHT_CUTS)):
            ring_step(hop, *weight_args(index))

    def proj_step(hop):
        ring_step(hop, *proj_args)

    def proj_arrival(slot):
        return proj_sem.at[slot]

    proj_args = (proj_block, proj_arrival, proj_sent, proj_arrival)

    def scatter(source, target, sent, arrival):
        def one(step, carry):
            device = lax.rem(me + step, DP)
            pltpu.make_async_remote_copy(
                src_ref=source.at[device],
                dst_ref=target.at[me],
                send_sem=sent,
                recv_sem=arrival,
                device_id={"dp": device},
                device_id_type=MESH,
            ).start()
            return carry

        lax.fori_loop(1, DP, one, 0)

    def weight_start():
        for index in range(len(WEIGHT_CUTS)):
            ring_start(*weight_args(index))

    @pl.when(section >= PLACERS)
    def _():
        ring_start(*proj_args)

    @pl.when(section < PLACERS)
    def _():
        weight_start()

    row = iota((HALF - SAMP * SLOT, HALF), 0)
    table = jnp.where(row < SAMP, spread(row, offset), spread(row - SAMP, count))
    table = table.astype(F32).astype(BF16)
    place, lane = iota((DP * 16, HALF), 0), iota((DP * 16, HALF), 1)
    is_row = lane < SAMP * SLOT
    lane_sample = jnp.where(is_row, lax.shift_right_logical(lane, 3), lane & 7)
    lane_inner = jnp.where(is_row, lane & 7, lax.shift_right_logical(lane, 3))
    picks = (
        (lax.shift_right_logical(place, 4) == spread(lane_sample, dest))
        & ((place & 15) == lane_inner)
        & (lane < SAMP * SLOT + 2 * SAMP)
    )
    load_vision.wait()
    slots = jnp.dot(
        picks.astype(F32).astype(BF16),
        jnp.concatenate([vision_part[...], table], axis=0),
        preferred_element_type=F32,
    )
    outgoing[...] = slots.astype(BF16).reshape(DP, 16, HALF)
    arrived[me] = outgoing[me]
    scatter(outgoing, arrived, route_sent, route_sem)
    load_gain.wait()

    def of_sources():
        message = arrived[:, SLOT : SLOT + 2, :].astype(F32).astype(jnp.int32)
        return message[:, 0:1], message[:, 1:2]

    def gather_piece(step):
        return pltpu.make_async_remote_copy(
            src_ref=pieces.at[piece],
            dst_ref=pieces.at[piece],
            send_sem=pieces_sent.at[step - 1],
            recv_sem=pieces_sem.at[step - 1],
            device_id={"tensor": lax.rem(tensor + step, PEERS)},
            device_id_type=MESH,
        )

    def pack():
        wait_bytes(arrived.at[pl.ds(0, DP - 1)], route_sem)
        start_row, row_count = of_sources()
        shape = (DP, 16, HALF)
        inner, column = iota(shape, 1), iota(shape, 2)
        gathers = (
            (lax.shift_right_logical(start_row, 5) == lax.shift_right_logical(column, 3))
            & (inner == (column & 7))
            & (inner < row_count)
        )
        packed = lax.dot_general(
            gathers.astype(F32).astype(BF16).reshape(DP * 16, HALF),
            arrived[...].reshape(DP * 16, HALF),
            (((0,), (0,)), ((), ())),
            preferred_element_type=F32,
        )
        pieces[piece] = packed[: SAMP * SLOT].astype(BF16)
        for step in range(1, PEERS):
            gather_piece(step).start()

    def gather_rows(step):
        mine = pieces.at[pl.ds(section * PEERS, PEERS)]
        return pltpu.make_async_remote_copy(
            src_ref=mine,
            dst_ref=mine,
            send_sem=rows_sent.at[step - 1],
            recv_sem=rows_sem.at[step - 1],
            device_id={"section": lax.rem(section + step, SECTIONS)},
            device_id_type=MESH,
        )

    def pass_pieces():
        for step in range(1, PEERS):
            gather_piece(step).wait_recv()
        for step in range(1, SECTIONS):

            @pl.when(lax.rem(section + step, SECTIONS) >= PLACERS)
            def _():
                gather_rows(step).start()

    def hand_in(source, half):
        part = images.at[source, pl.ds(half * SAMP * SLOT // 2, SAMP * SLOT // 2)]
        return pltpu.make_async_remote_copy(
            src_ref=part,
            dst_ref=part,
            send_sem=images_sent.at[half],
            recv_sem=images_sem.at[source, half],
            device_id={"section": 0},
            device_id_type=MESH,
        )

    def times_columns(offsets):
        total = None
        for step in offsets:
            there = lax.rem(chip + CHIPS + step, CHIPS)
            other = there * 2 + 1 - core
            landed(proj_block(other), proj_sent, proj_arrival(other))
            term = jnp.dot(
                pieces[there],
                proj_ring[pl.ds(there * 2, 2)].reshape(2 * depth, FRONT),
                preferred_element_type=F32,
            )
            total = term if total is None else total + term
        return total

    def doc_tables():
        start_row, row_count = of_sources()
        start_row, row_count = start_row[:, 0], row_count[:, 0]
        mark = iota((DP, HALF), 1)
        of_doc = lax.shift_right_logical(start_row, 5) == lax.shift_right_logical(mark, 3)
        doc_row = jnp.sum(jnp.where(of_doc, start_row, 0), axis=0, keepdims=True)
        doc_count = jnp.sum(jnp.where(of_doc, row_count, 0), axis=0, keepdims=True)
        return doc_row, doc_count

    def place(micro, half, doc_row, doc_count):
        known = slice(half * SAMP * SLOT // 2, (half + 1) * SAMP * SLOT // 2)
        row, mark = iota((ROWS, HALF), 0) + micro * ROWS, iota((ROWS, HALF), 1)
        puts = (row == doc_row + (mark & 7)) & ((mark & 7) < doc_count) & (mark < SAMP * SLOT)
        puts = puts.astype(F32)
        taken = jnp.sum(puts, axis=1, keepdims=True) > 0.0
        puts = puts[:, known].astype(BF16)
        here = pl.ds(pl.multiple_of(micro * ROWS, ROWS), ROWS)
        placed = [
            jnp.dot(
                puts,
                images[source, known, part * HALF : (part + 1) * HALF],
                preferred_element_type=F32,
            )
            for source, part in IMAGE_TILES
        ]
        placed = jnp.concatenate(placed, axis=1)
        hidden[here] = jnp.where(taken, placed, hidden[here].astype(F32)).astype(BF16)

    def prepare_back():
        load_cotangent.wait()
        start_row, row_count = of_sources()
        total = text.shape[0]
        start_row = jnp.concatenate([start_row] * (total // HALF), axis=2)
        row_count = jnp.concatenate([row_count] * (total // HALF), axis=2)
        shape = (DP, SLOT, total)
        inner, row = iota(shape, 1), iota(shape, 2)
        takes = (start_row + inner == row) & (inner < row_count)
        rows = jnp.dot(
            takes.astype(F32).reshape(DP * SLOT, total).astype(BF16),
            cotangent[...],
            preferred_element_type=F32,
        ).reshape(DP, SLOT, width)
        tiles = [rows[:, :, first : first + HALF] for first in range(0, width, HALF)]
        spare = jnp.zeros((DP, FOLDED - SLOT * len(tiles), HALF), F32)
        returning[...] = jnp.concatenate(tiles + [spare], axis=1).astype(BF16)
        back[me] = returning[me]

    def exchange(step):
        return pltpu.make_async_remote_copy(
            src_ref=image_grad,
            dst_ref=image_grad,
            send_sem=grads_sent.at[step - 1],
            recv_sem=grads_sem,
            device_id={"section": step},
            device_id_type=MESH,
        )

    def collect():
        wait_bytes(back.at[pl.ds(0, DP - 1)], back_sem)
        found = [back[dest[i]].astype(F32) for i in range(SAMP)]
        for tile in range(width // HALF):
            rows = [each[tile * SLOT : (tile + 1) * SLOT] for each in found]
            image_grad[:, tile * HALF : (tile + 1) * HALF] = jnp.concatenate(
                rows, axis=0
            ).astype(BF16)
        for step in range(1, SECTIONS):
            exchange(step).start()

    def rows_of(micro):
        return pl.ds(pl.multiple_of(micro * ROWS, ROWS), ROWS)

    def store(micro):
        return pltpu.make_async_copy(
            out.at[rows_of(micro)], out_result.at[rows_of(micro)], store_sem.at[micro]
        )

    def relay(micro):
        return pltpu.make_async_remote_copy(
            src_ref=out.at[rows_of(micro)],
            dst_ref=hidden.at[rows_of(micro)],
            send_sem=out_sent.at[micro],
            recv_sem=hidden_sem.at[micro],
            device_id={"section": following},
            device_id_type=MESH,
        )

    def share(micro, step):
        return pltpu.make_async_remote_copy(
            src_ref=mixed.at[tensor, rows_of(micro)],
            dst_ref=mixed.at[tensor, rows_of(micro)],
            send_sem=mixed_sent.at[micro, step - 1],
            recv_sem=mixed_sem.at[micro, step - 1],
            device_id={"tensor": lax.rem(tensor + step, PEERS)},
            device_id_type=MESH,
        )

    def mix(micro):
        mixed[tensor, rows_of(micro)] = attend(hidden[rows_of(micro)], gain[...])
        for step in (1, 3, 2):
            share(micro, step).start()

    def project(micro):
        total = hidden[rows_of(micro)].astype(F32)
        for step in (0, 1, 3, 2):
            if step > 0:
                share(micro, step).wait_recv()
            peer = lax.rem(tensor + PEERS - step, PEERS)
            total += jnp.dot(
                mixed[peer, rows_of(micro)],
                weight[pl.ds(pl.multiple_of(peer * width, HEAD), width)],
                preferred_element_type=F32,
            )
        out[rows_of(micro)] = total.astype(BF16)
        store(micro).start()

        @pl.when(section < SECTIONS - 1)
        def _():
            relay(micro).start()

    def mix_some(half):
        for source in range(PLACERS, SECTIONS):
            hand_in(source, half).wait_recv()
        doc_row, doc_count = doc_tables()

        def one(micro, carry):
            place(micro, half, doc_row, doc_count)
            mix(micro)
            return carry

        lax.fori_loop(half * micros // 2, (half + 1) * micros // 2, one, 0)

    @pl.when(section < PLACERS)
    def _():
        weight_step(1)
        weight_step(2)
        pack()
        weight_step(3)
        pass_pieces()
        weight_step(4)

        @pl.when(section == 0)
        def _():
            prepare_back()

        for hop in range(5, 8):
            weight_step(hop)

    @pl.when(section == 0)
    def _():
        load_text.wait()
        mix_some(0)

    @pl.when(section < PLACERS)
    def _():
        weight_step(8)

    @pl.when(section == 0)
    def _():
        mix_some(1)

    @pl.when(section >= PLACERS)
    def _():
        def weight_early(hop, first):
            @pl.when(section == first)
            def _():
                if hop == 0:
                    weight_start()
                else:
                    weight_step(hop)

        proj_step(1)
        weight_early(0, 2)
        proj_step(2)
        proj_step(3)
        weight_early(0, 3)
        pack()
        proj_step(4)
        weight_early(1, 2)
        pass_pieces()
        proj_step(5)
        proj_step(6)
        weight_early(2, 2)
        weight_early(1, 3)
        for step in range(1, SECTIONS):
            gather_rows(step).wait_recv()
        total = times_columns((0, 1, -1, 2, -2, 3, -3, 4, -4, 5, -5))
        proj_step(7)
        total += times_columns((6, -6))
        proj_step(8)
        weight_early(3, 2)
        weight_early(2, 3)
        total += times_columns((7, -7, 8))
        images[section] = total.astype(BF16)
        for half in range(2):
            hand_in(section, half).start()
        weight_early(3, 3)
        for hop in range(4, 9):
            weight_step(hop)

    wait_bytes(weight.at[pl.ds(0, CHIPS * share_rows)], weight_near)

    def step(turn, carry):
        @pl.when((section > 0) & (turn < micros))
        def _():
            relay(turn).wait_recv()
            mix(turn)

        @pl.when(turn > 1)
        def _():
            project(turn - 2)

        @pl.when((section == 0) & (turn == BACK_TURN))
        def _():
            scatter(returning, back, back_sent, back_sem)

        return carry

    lax.fori_loop(0, micros + 2, step, 0)

    @pl.when(section == 0)
    def _():
        collect()
        wait_bytes(returning.at[pl.ds(0, DP - 1)], back_sent)
        for step in range(1, SECTIONS):
            exchange(step).wait_send()

    @pl.when(section > 0)
    def _():
        exchange(1).wait_recv()

    store_grad = pltpu.make_async_copy(image_grad, image_grad_result, store_grad_sem)
    store_grad.start()

    wait_bytes(weight.at[pl.ds(0, (DP - 1) * share_rows)], weight_sent)
    wait_bytes(arrived.at[pl.ds(0, DP - 1)], route_sent)

    @pl.when(section >= PLACERS)
    def _():
        wait_bytes(proj_ring.at[pl.ds(0, DP - 1)], proj_sent)
        for half in range(2):
            hand_in(section, half).wait_send()

    for step in range(1, PEERS):
        gather_piece(step).wait_send()
    for step in range(1, SECTIONS):

        @pl.when(lax.rem(section + step, SECTIONS) >= PLACERS)
        def _():
            gather_rows(step).wait_send()

    def drain(micro, carry):
        store(micro).wait()
        for step in range(1, PEERS):
            share(micro, step).wait_send()

        @pl.when(section < SECTIONS - 1)
        def _():
            relay(micro).wait_send()

        return carry

    lax.fori_loop(0, micros, drain, 0)
    store_grad.wait()


def on_device(
    text_embed,
    vision,
    proj_weight,
    out_weight,
    qk_gain,
    image_counts,
    sample_shard,
    sample_offset,
    embed_grad,
):
    rows, width = text_embed.shape
    micros = rows // ROWS
    depth = proj_weight.shape[0]
    hbm = pl.BlockSpec(memory_space=pl.ANY)
    smem = pl.BlockSpec(memory_space=pltpu.SMEM)
    dma = pltpu.SemaphoreType.DMA
    outputs, image_grad = pl.pallas_call(
        whole_kernel,
        out_shape=(
            jax.ShapeDtypeStruct((rows, width), BF16),
            jax.ShapeDtypeStruct((vision.shape[0], width), BF16),
        ),
        in_specs=[hbm] * 5 + [smem] * 3 + [hbm],
        out_specs=(hbm, hbm),
        scratch_shapes=[
            pltpu.VMEM((rows, width), BF16),
            pltpu.VMEM((vision.shape[0], width), BF16),
            pltpu.VMEM((1, width), F32),
            pltpu.VMEM((vision.shape[0], HALF), BF16),
            pltpu.VMEM((rows, width), BF16),
            pltpu.VMEM((DP, depth, FRONT), BF16),
            pltpu.VMEM((DP * out_weight.shape[1], width), BF16),
            pltpu.VMEM((DP, 16, HALF), BF16),
            pltpu.VMEM((DP, 16, HALF), BF16),
            pltpu.VMEM((PIECES, SAMP * SLOT, HALF), BF16),
            pltpu.VMEM((SECTIONS, SAMP * SLOT, FRONT), BF16),
            pltpu.VMEM((DP, FOLDED, HALF), BF16),
            pltpu.VMEM((DP, FOLDED, HALF), BF16),
            pltpu.VMEM((rows, width), BF16),
            pltpu.VMEM((PEERS, rows, width), BF16),
            dma((6,)),
            dma((micros,)),
            dma,
            dma((PEERS - 1,)),
            dma((PEERS - 1,)),
            dma((SECTIONS - 1,)),
            dma((SECTIONS - 1,)),
            dma((DP,)),
            dma,
            dma((len(WEIGHT_CUTS), DP)),
            dma,
            dma,
            dma,
            dma,
            dma,
            dma,
            dma((SECTIONS, 2)),
            dma((2,)),
            dma,
            dma((SECTIONS - 1,)),
            dma((micros,)),
            dma((micros, PEERS - 1)),
            dma((micros,)),
            dma((micros, PEERS - 1)),
        ],
        compiler_params=pltpu.CompilerParams(
            collective_id=0, has_side_effects=True, vmem_limit_bytes=60 * 1024 * 1024
        ),
    )(
        text_embed,
        vision,
        proj_weight,
        out_weight[0],
        qk_gain,
        image_counts,
        sample_shard,
        sample_offset,
        embed_grad,
    )
    return (outputs[None], image_grad)


def solution(mesh):
    placed = (
        P("dp", "tensor"),
        P("dp", None),
        P("dp", "tensor"),
        P("section", "dp", "tensor"),
        P("section", "tensor"),
        P("dp"),
        P("dp"),
        P("dp"),
        P("dp", "tensor"),
    )
    return jax.shard_map(
        on_device,
        mesh=mesh,
        in_specs=placed,
        out_specs=(P("section", "dp", "tensor"), P("dp", "tensor")),
        check_vma=False,
    )
```

```python
import jax
import jax.numpy as jnp
from jax import lax
from jax.experimental import pallas as pl
from jax.experimental.pallas import tpu as pltpu
from jax.sharding import PartitionSpec as P

HEAD = 128
DOC = 32
SLOT = 8
SAMP = 8
ROWS = 32
SECTIONS = 4
PEERS = 4
DP = 32
CHIPS = 16
PIECES = 16
HALF = 128
FRONT = 512
FOLDED = 64
BACK_TURN = 4
PLACERS = 2
WEIGHT_CUTS = ((0, 64), (64, 48))
IMAGE_TILES = ((2, 0), (2, 1), (2, 2), (2, 3), (3, 1), (3, 2), (3, 3))
TILES = ((1, 0), (1, 1), (2, 0), (2, 1), (3, 0), (3, 1), (3, 2))
MESH = pl.DeviceIdType.MESH
BF16 = jnp.bfloat16
F32 = jnp.float32


def attend(x, gains):
    rows = x.shape[0]
    row, col = iota((rows, rows), 0), iota((rows, rows), 1)
    allowed = (col <= row) & (lax.div(col, DOC) == lax.div(row, DOC))
    cuts = [slice(first, first + HEAD) for first in range(0, x.shape[1], HEAD)]
    values = [x[:, cut] for cut in cuts]
    wide = [value.astype(F32) for value in values]
    means = [jnp.mean(value * value, axis=-1, keepdims=True) for value in wide]
    normed = [
        (value * lax.rsqrt(mean + 1e-06) * gains[:, cut]).astype(BF16)
        for value, mean, cut in zip(wide, means, cuts)
    ]
    scores = [
        lax.dot_general(each, each, (((1,), (1,)), ((), ())), preferred_element_type=F32)
        for each in normed
    ]
    weights = [jnp.where(allowed, jnp.exp(score * (2.0 / HEAD)), 0.0) for score in scores]
    weights = [(each / jnp.sum(each, axis=-1, keepdims=True)).astype(BF16) for each in weights]
    mixed = [
        jnp.dot(each, value, preferred_element_type=F32).astype(BF16)
        for each, value in zip(weights, values)
    ]
    return jnp.concatenate(mixed, axis=1)


def iota(shape, dim):
    return lax.broadcasted_iota(jnp.int32, shape, dim)


def spread(index, scalars):
    total = jnp.zeros(index.shape, jnp.int32)
    for i in range(SAMP):
        total = jnp.where(index == i, scalars[i], total)
    return total


def wait_bytes(ref, sem):
    pltpu.make_async_copy(ref, ref, sem).wait()


def whole_kernel(
    text,
    vision,
    proj,
    shard_weight,
    gain_input,
    counts,
    dests,
    offsets,
    cotangent_input,
    out_result,
    image_grad_result,
    out,
    image_grad,
    gain,
    vision_part,
    cotangent,
    proj_ring,
    weight,
    outgoing,
    arrived,
    pieces,
    images,
    returning,
    back,
    hidden,
    mixed,
    load_sem,
    store_sem,
    store_grad_sem,
    pieces_sem,
    pieces_sent,
    rows_sem,
    rows_sent,
    proj_sem,
    proj_sent,
    weight_sem,
    weight_near,
    weight_sent,
    route_sem,
    route_sent,
    back_sem,
    back_sent,
    images_sem,
    images_sent,
    grads_sem,
    grads_sent,
    hidden_sem,
    mixed_sem,
    out_sent,
    mixed_sent,
):
    section, tensor = lax.axis_index("section"), lax.axis_index("tensor")
    me = lax.axis_index("dp")
    chip, core = lax.div(me, 2), lax.rem(me, 2)
    width = hidden.shape[1]
    micros = hidden.shape[0] // ROWS
    following = lax.rem(section + 1, SECTIONS)
    right = lax.rem(chip + 1, CHIPS) * 2 + core
    left = lax.rem(chip + CHIPS - 1, CHIPS) * 2 + core
    near = chip * 2 + 1 - core
    image_column = pl.multiple_of(lax.div(section, 3) * 3 * HALF, HALF)
    piece = section * PEERS + tensor
    depth, share_rows = proj.shape[0], shard_weight.shape[0]

    def load(source, target, index):
        return pltpu.make_async_copy(source, target, load_sem.at[index])

    own = pl.multiple_of(me * share_rows, 16)
    load_weight = load(shard_weight, weight.at[pl.ds(own, share_rows)], 0)
    load_vision = load(
        vision.at[:, pl.ds(pl.multiple_of(piece * HALF, HALF), HALF)], vision_part, 1
    )
    load_cotangent = load(cotangent_input, cotangent, 2)
    load_text = load(text, hidden, 3)
    load_proj = load(proj.at[:, pl.ds(image_column, FRONT)], proj_ring.at[me], 4)
    load_gain = load(gain_input, gain, 5)
    load_weight.start()
    load_gain.start()
    load_vision.start()

    @pl.when(section >= PLACERS)
    def _():
        load_proj.start()

    barrier = pltpu.get_barrier_semaphore()

    def greet(step, carry):
        pl.semaphore_signal(
            barrier, inc=1, device_id={"dp": lax.rem(me + step, DP)}, device_id_type=MESH
        )
        return carry

    lax.fori_loop(1, DP, greet, 0)
    for step in range(1, 4):
        pl.semaphore_signal(
            barrier, inc=1, device_id={"tensor": lax.rem(tensor + step, PEERS)}, device_id_type=MESH
        )
        pl.semaphore_signal(
            barrier,
            inc=1,
            device_id={"section": lax.rem(section + step, SECTIONS)},
            device_id_type=MESH,
        )

    @pl.when(section == 0)
    def _():
        load_text.start()
        load_cotangent.start()

    dest = [dests[i] for i in range(SAMP)]
    offset = [offsets[i] for i in range(SAMP)]
    count = [counts[i] for i in range(SAMP)]

    load_weight.wait()

    @pl.when(section >= PLACERS)
    def _():
        load_proj.wait()

    pl.semaphore_wait(barrier, DP - 1 + 6)

    def send(ref, sent, arrival, device):
        pltpu.make_async_remote_copy(
            src_ref=ref,
            dst_ref=ref,
            send_sem=sent,
            recv_sem=arrival,
            device_id={"dp": device},
            device_id_type=MESH,
        ).start()

    def landed(ref, sent, arrival):
        pltpu.make_async_remote_copy(
            src_ref=ref,
            dst_ref=ref,
            send_sem=sent,
            recv_sem=arrival,
            device_id={"dp": near},
            device_id_type=MESH,
        ).wait_recv()

    def proj_block(slot):
        return proj_ring.at[slot]

    def weight_block(slot, cut):
        start = pl.multiple_of(slot * share_rows + cut[0], 16)
        return weight.at[pl.ds(start, cut[1])]

    def ring_start(block, arrival, sent, near_at):
        for device in (right, left):
            send(block(me), sent, arrival(me), device)
        send(block(me), sent, near_at(me), near)

    def ring_step(hop, block, arrival, sent, near_at):
        from_left = lax.rem(chip + CHIPS - hop, CHIPS) * 2 + core
        from_right = lax.rem(chip + hop, CHIPS) * 2 + core
        if hop < CHIPS // 2:
            landed(block(from_left), sent, arrival(from_left))
            if hop < CHIPS // 2 - 1:
                send(block(from_left), sent, arrival(from_left), right)
            else:

                @pl.when(core == 0)
                def _():
                    send(block(from_left), sent, arrival(from_left), right)

            landed(block(from_right), sent, arrival(from_right))
            if hop < CHIPS // 2 - 1:
                send(block(from_right), sent, arrival(from_right), left)
            else:

                @pl.when(core == 1)
                def _():
                    send(block(from_right), sent, arrival(from_right), left)

            send(block(from_left), sent, near_at(from_left), near)
            send(block(from_right), sent, near_at(from_right), near)
        else:
            landed(block(from_left), sent, arrival(from_left))
            send(block(from_left), sent, near_at(from_left), near)

    def weight_args(index):
        cut = WEIGHT_CUTS[index]
        return (
            lambda slot: weight_block(slot, cut),
            lambda slot: weight_sem.at[index, slot],
            weight_sent,
            lambda slot: weight_near,
        )

    def weight_step(hop):
        for index in range(len(WEIGHT_CUTS)):
            ring_step(hop, *weight_args(index))

    def proj_step(hop):
        ring_step(hop, *proj_args)

    def proj_arrival(slot):
        return proj_sem.at[slot]

    proj_args = (proj_block, proj_arrival, proj_sent, proj_arrival)

    def scatter(source, target, sent, arrival):
        def one(step, carry):
            device = lax.rem(me + step, DP)
            pltpu.make_async_remote_copy(
                src_ref=source.at[device],
                dst_ref=target.at[me],
                send_sem=sent,
                recv_sem=arrival,
                device_id={"dp": device},
                device_id_type=MESH,
            ).start()
            return carry

        lax.fori_loop(1, DP, one, 0)

    def weight_start():
        for index in range(len(WEIGHT_CUTS)):
            ring_start(*weight_args(index))

    @pl.when(section >= PLACERS)
    def _():
        ring_start(*proj_args)

    @pl.when(section < PLACERS)
    def _():
        weight_start()

    row = iota((HALF - SAMP * SLOT, HALF), 0)
    table = jnp.where(row < SAMP, spread(row, offset), spread(row - SAMP, count))
    table = table.astype(F32).astype(BF16)
    place, lane = iota((DP * 16, HALF), 0), iota((DP * 16, HALF), 1)
    is_row = lane < SAMP * SLOT
    lane_sample = jnp.where(is_row, lax.shift_right_logical(lane, 3), lane & 7)
    lane_inner = jnp.where(is_row, lane & 7, lax.shift_right_logical(lane, 3))
    picks = (
        (lax.shift_right_logical(place, 4) == spread(lane_sample, dest))
        & ((place & 15) == lane_inner)
        & (lane < SAMP * SLOT + 2 * SAMP)
    )
    load_vision.wait()
    slots = jnp.dot(
        picks.astype(F32).astype(BF16),
        jnp.concatenate([vision_part[...], table], axis=0),
        preferred_element_type=F32,
    )
    outgoing[...] = slots.astype(BF16).reshape(DP, 16, HALF)
    arrived[me] = outgoing[me]
    scatter(outgoing, arrived, route_sent, route_sem)
    load_gain.wait()

    def of_sources():
        message = arrived[:, SLOT : SLOT + 2, :].astype(F32).astype(jnp.int32)
        return message[:, 0:1], message[:, 1:2]

    def gather_piece(step):
        return pltpu.make_async_remote_copy(
            src_ref=pieces.at[piece],
            dst_ref=pieces.at[piece],
            send_sem=pieces_sent.at[step - 1],
            recv_sem=pieces_sem.at[step - 1],
            device_id={"tensor": lax.rem(tensor + step, PEERS)},
            device_id_type=MESH,
        )

    def pack():
        wait_bytes(arrived.at[pl.ds(0, DP - 1)], route_sem)
        start_row, row_count = of_sources()
        shape = (DP, 16, HALF)
        inner, column = iota(shape, 1), iota(shape, 2)
        gathers = (
            (lax.shift_right_logical(start_row, 5) == lax.shift_right_logical(column, 3))
            & (inner == (column & 7))
            & (inner < row_count)
        )
        packed = lax.dot_general(
            gathers.astype(F32).astype(BF16).reshape(DP * 16, HALF),
            arrived[...].reshape(DP * 16, HALF),
            (((0,), (0,)), ((), ())),
            preferred_element_type=F32,
        )
        pieces[piece] = packed[: SAMP * SLOT].astype(BF16)
        for step in range(1, PEERS):
            gather_piece(step).start()

    def gather_rows(step):
        mine = pieces.at[pl.ds(section * PEERS, PEERS)]
        return pltpu.make_async_remote_copy(
            src_ref=mine,
            dst_ref=mine,
            send_sem=rows_sent.at[step - 1],
            recv_sem=rows_sem.at[step - 1],
            device_id={"section": lax.rem(section + step, SECTIONS)},
            device_id_type=MESH,
        )

    def pass_pieces():
        for step in range(1, PEERS):
            gather_piece(step).wait_recv()
        for step in range(1, SECTIONS):

            @pl.when(lax.rem(section + step, SECTIONS) >= PLACERS)
            def _():
                gather_rows(step).start()

    def hand_in(source, half):
        part = images.at[source, pl.ds(half * SAMP * SLOT // 2, SAMP * SLOT // 2)]
        return pltpu.make_async_remote_copy(
            src_ref=part,
            dst_ref=part,
            send_sem=images_sent.at[half],
            recv_sem=images_sem.at[source, half],
            device_id={"section": 0},
            device_id_type=MESH,
        )

    def times_columns(offsets):
        total = None
        for step in offsets:
            there = lax.rem(chip + CHIPS + step, CHIPS)
            other = there * 2 + 1 - core
            landed(proj_block(other), proj_sent, proj_arrival(other))
            term = jnp.dot(
                pieces[there],
                proj_ring[pl.ds(there * 2, 2)].reshape(2 * depth, FRONT),
                preferred_element_type=F32,
            )
            total = term if total is None else total + term
        return total

    def doc_tables():
        start_row, row_count = of_sources()
        start_row, row_count = start_row[:, 0], row_count[:, 0]
        mark = iota((DP, HALF), 1)
        of_doc = lax.shift_right_logical(start_row, 5) == lax.shift_right_logical(mark, 3)
        doc_row = jnp.sum(jnp.where(of_doc, start_row, 0), axis=0, keepdims=True)
        doc_count = jnp.sum(jnp.where(of_doc, row_count, 0), axis=0, keepdims=True)
        return doc_row, doc_count

    def place(micro, half, doc_row, doc_count):
        known = slice(half * SAMP * SLOT // 2, (half + 1) * SAMP * SLOT // 2)
        row, mark = iota((ROWS, HALF), 0) + micro * ROWS, iota((ROWS, HALF), 1)
        puts = (row == doc_row + (mark & 7)) & ((mark & 7) < doc_count) & (mark < SAMP * SLOT)
        puts = puts.astype(F32)
        taken = jnp.sum(puts, axis=1, keepdims=True) > 0.0
        puts = puts[:, known].astype(BF16)
        here = pl.ds(pl.multiple_of(micro * ROWS, ROWS), ROWS)
        placed = [
            jnp.dot(
                puts,
                images[source, known, part * HALF : (part + 1) * HALF],
                preferred_element_type=F32,
            )
            for source, part in IMAGE_TILES
        ]
        placed = jnp.concatenate(placed, axis=1)
        hidden[here] = jnp.where(taken, placed, hidden[here].astype(F32)).astype(BF16)

    def prepare_back():
        load_cotangent.wait()
        start_row, row_count = of_sources()
        total = text.shape[0]
        start_row = jnp.concatenate([start_row] * (total // HALF), axis=2)
        row_count = jnp.concatenate([row_count] * (total // HALF), axis=2)
        shape = (DP, SLOT, total)
        inner, row = iota(shape, 1), iota(shape, 2)
        takes = (start_row + inner == row) & (inner < row_count)
        rows = jnp.dot(
            takes.astype(F32).reshape(DP * SLOT, total).astype(BF16),
            cotangent[...],
            preferred_element_type=F32,
        ).reshape(DP, SLOT, width)
        tiles = [rows[:, :, first : first + HALF] for first in range(0, width, HALF)]
        spare = jnp.zeros((DP, FOLDED - SLOT * len(tiles), HALF), F32)
        returning[...] = jnp.concatenate(tiles + [spare], axis=1).astype(BF16)
        back[me] = returning[me]

    def exchange(step):
        return pltpu.make_async_remote_copy(
            src_ref=image_grad,
            dst_ref=image_grad,
            send_sem=grads_sent.at[step - 1],
            recv_sem=grads_sem,
            device_id={"section": step},
            device_id_type=MESH,
        )

    def collect():
        wait_bytes(back.at[pl.ds(0, DP - 1)], back_sem)
        found = [back[dest[i]].astype(F32) for i in range(SAMP)]
        for tile in range(width // HALF):
            rows = [each[tile * SLOT : (tile + 1) * SLOT] for each in found]
            image_grad[:, tile * HALF : (tile + 1) * HALF] = jnp.concatenate(
                rows, axis=0
            ).astype(BF16)
        for step in range(1, SECTIONS):
            exchange(step).start()

    def rows_of(micro):
        return pl.ds(pl.multiple_of(micro * ROWS, ROWS), ROWS)

    def store(micro):
        return pltpu.make_async_copy(
            out.at[rows_of(micro)], out_result.at[rows_of(micro)], store_sem.at[micro]
        )

    def relay(micro):
        return pltpu.make_async_remote_copy(
            src_ref=out.at[rows_of(micro)],
            dst_ref=hidden.at[rows_of(micro)],
            send_sem=out_sent.at[micro],
            recv_sem=hidden_sem.at[micro],
            device_id={"section": following},
            device_id_type=MESH,
        )

    def share(micro, step):
        return pltpu.make_async_remote_copy(
            src_ref=mixed.at[tensor, rows_of(micro)],
            dst_ref=mixed.at[tensor, rows_of(micro)],
            send_sem=mixed_sent.at[micro, step - 1],
            recv_sem=mixed_sem.at[micro, step - 1],
            device_id={"tensor": lax.rem(tensor + step, PEERS)},
            device_id_type=MESH,
        )

    def mix(micro):
        mixed[tensor, rows_of(micro)] = attend(hidden[rows_of(micro)], gain[...])
        for step in (1, 3, 2):
            share(micro, step).start()

    def project(micro):
        total = hidden[rows_of(micro)].astype(F32)
        for step in (0, 1, 3, 2):
            if step > 0:
                share(micro, step).wait_recv()
            peer = lax.rem(tensor + PEERS - step, PEERS)
            total += jnp.dot(
                mixed[peer, rows_of(micro)],
                weight[pl.ds(pl.multiple_of(peer * width, HEAD), width)],
                preferred_element_type=F32,
            )
        out[rows_of(micro)] = total.astype(BF16)

        @pl.when(section < SECTIONS - 1)
        def _():
            relay(micro).start()

        store(micro).start()

    def mix_some(half):
        for source in range(PLACERS, SECTIONS):
            hand_in(source, half).wait_recv()
        doc_row, doc_count = doc_tables()

        def one(micro, carry):
            place(micro, half, doc_row, doc_count)
            mix(micro)
            return carry

        lax.fori_loop(half * micros // 2, (half + 1) * micros // 2, one, 0)

    @pl.when(section < PLACERS)
    def _():
        weight_step(1)
        weight_step(2)
        pack()
        weight_step(3)
        pass_pieces()
        weight_step(4)

        @pl.when(section == 0)
        def _():
            prepare_back()

        for hop in range(5, 8):
            weight_step(hop)

    @pl.when(section == 0)
    def _():
        load_text.wait()
        mix_some(0)

    @pl.when(section < PLACERS)
    def _():
        weight_step(8)

    @pl.when(section == 0)
    def _():
        mix_some(1)

    @pl.when(section >= PLACERS)
    def _():
        def weight_early(hop, first):
            @pl.when(section == first)
            def _():
                if hop == 0:
                    weight_start()
                else:
                    weight_step(hop)

        proj_step(1)
        weight_early(0, 2)
        proj_step(2)
        proj_step(3)
        weight_early(0, 3)
        pack()
        proj_step(4)
        weight_early(1, 2)
        pass_pieces()
        proj_step(5)
        proj_step(6)
        weight_early(2, 2)
        weight_early(1, 3)
        for step in range(1, SECTIONS):
            gather_rows(step).wait_recv()
        total = times_columns((0, 1, -1, 2, -2, 3, -3, 4, -4, 5, -5))
        proj_step(7)
        total += times_columns((6, -6))
        proj_step(8)
        weight_early(3, 2)
        weight_early(2, 3)
        total += times_columns((7, -7, 8))
        images[section] = total.astype(BF16)
        for half in range(2):
            hand_in(section, half).start()
        weight_early(3, 3)
        for hop in range(4, 9):
            weight_step(hop)

    wait_bytes(weight.at[pl.ds(0, CHIPS * share_rows)], weight_near)

    def step(turn, carry):
        @pl.when((section > 0) & (turn < micros))
        def _():
            relay(turn).wait_recv()
            mix(turn)

        @pl.when(turn > 1)
        def _():
            project(turn - 2)

        @pl.when((section == 0) & (turn == BACK_TURN))
        def _():
            scatter(returning, back, back_sent, back_sem)

        return carry

    lax.fori_loop(0, micros + 2, step, 0)

    @pl.when(section == 0)
    def _():
        collect()
        wait_bytes(returning.at[pl.ds(0, DP - 1)], back_sent)
        for step in range(1, SECTIONS):
            exchange(step).wait_send()

    @pl.when(section > 0)
    def _():
        exchange(1).wait_recv()

    store_grad = pltpu.make_async_copy(image_grad, image_grad_result, store_grad_sem)
    store_grad.start()

    wait_bytes(weight.at[pl.ds(0, (DP - 1) * share_rows)], weight_sent)
    wait_bytes(arrived.at[pl.ds(0, DP - 1)], route_sent)

    @pl.when(section >= PLACERS)
    def _():
        wait_bytes(proj_ring.at[pl.ds(0, DP - 1)], proj_sent)
        for half in range(2):
            hand_in(section, half).wait_send()

    for step in range(1, PEERS):
        gather_piece(step).wait_send()
    for step in range(1, SECTIONS):

        @pl.when(lax.rem(section + step, SECTIONS) >= PLACERS)
        def _():
            gather_rows(step).wait_send()

    def drain(micro, carry):
        store(micro).wait()
        for step in range(1, PEERS):
            share(micro, step).wait_send()

        @pl.when(section < SECTIONS - 1)
        def _():
            relay(micro).wait_send()

        return carry

    lax.fori_loop(0, micros, drain, 0)
    store_grad.wait()


def on_device(
    text_embed,
    vision,
    proj_weight,
    out_weight,
    qk_gain,
    image_counts,
    sample_shard,
    sample_offset,
    embed_grad,
):
    rows, width = text_embed.shape
    micros = rows // ROWS
    depth = proj_weight.shape[0]
    hbm = pl.BlockSpec(memory_space=pl.ANY)
    smem = pl.BlockSpec(memory_space=pltpu.SMEM)
    dma = pltpu.SemaphoreType.DMA
    outputs, image_grad = pl.pallas_call(
        whole_kernel,
        out_shape=(
            jax.ShapeDtypeStruct((rows, width), BF16),
            jax.ShapeDtypeStruct((vision.shape[0], width), BF16),
        ),
        in_specs=[hbm] * 5 + [smem] * 3 + [hbm],
        out_specs=(hbm, hbm),
        scratch_shapes=[
            pltpu.VMEM((rows, width), BF16),
            pltpu.VMEM((vision.shape[0], width), BF16),
            pltpu.VMEM((1, width), F32),
            pltpu.VMEM((vision.shape[0], HALF), BF16),
            pltpu.VMEM((rows, width), BF16),
            pltpu.VMEM((DP, depth, FRONT), BF16),
            pltpu.VMEM((DP * out_weight.shape[1], width), BF16),
            pltpu.VMEM((DP, 16, HALF), BF16),
            pltpu.VMEM((DP, 16, HALF), BF16),
            pltpu.VMEM((PIECES, SAMP * SLOT, HALF), BF16),
            pltpu.VMEM((SECTIONS, SAMP * SLOT, FRONT), BF16),
            pltpu.VMEM((DP, FOLDED, HALF), BF16),
            pltpu.VMEM((DP, FOLDED, HALF), BF16),
            pltpu.VMEM((rows, width), BF16),
            pltpu.VMEM((PEERS, rows, width), BF16),
            dma((6,)),
            dma((micros,)),
            dma,
            dma((PEERS - 1,)),
            dma((PEERS - 1,)),
            dma((SECTIONS - 1,)),
            dma((SECTIONS - 1,)),
            dma((DP,)),
            dma,
            dma((len(WEIGHT_CUTS), DP)),
            dma,
            dma,
            dma,
            dma,
            dma,
            dma,
            dma((SECTIONS, 2)),
            dma((2,)),
            dma,
            dma((SECTIONS - 1,)),
            dma((micros,)),
            dma((micros, PEERS - 1)),
            dma((micros,)),
            dma((micros, PEERS - 1)),
        ],
        compiler_params=pltpu.CompilerParams(
            collective_id=0, has_side_effects=True, vmem_limit_bytes=60 * 1024 * 1024
        ),
    )(
        text_embed,
        vision,
        proj_weight,
        out_weight[0],
        qk_gain,
        image_counts,
        sample_shard,
        sample_offset,
        embed_grad,
    )
    return (outputs[None], image_grad)


def solution(mesh):
    placed = (
        P("dp", "tensor"),
        P("dp", None),
        P("dp", "tensor"),
        P("section", "dp", "tensor"),
        P("section", "tensor"),
        P("dp"),
        P("dp"),
        P("dp"),
        P("dp", "tensor"),
    )
    return jax.shard_map(
        on_device,
        mesh=mesh,
        in_specs=placed,
        out_specs=(P("section", "dp", "tensor"), P("dp", "tensor")),
        check_vma=False,
    )
```
